512 devices in a mesh: dp: 32 (over z, core), fsdp: 16 (over x, y).
Axes of the slice: x: 4, y: 4, z: 16, core: 2. Of those that a mesh axis runs over, the one named last changes fastest.
Arguments:
- counts: int32 [512], P(('dp', 'fsdp')), may hold values from 1 to 4
- tokens: bfloat16 [65536, 8192], P(('dp', 'fsdp')), may hold values from -24 to 24
- queries: bfloat16 [65536, 4096], P(('dp', 'fsdp')), may hold values from -6 to 6
- values: bfloat16 [65536, 512], P(('dp', 'fsdp')), may hold values from -6 to 6
- out_grad: bfloat16 [65536, 4096], P(('dp', 'fsdp')), may hold values from -6 to 6
- key_codes: bfloat16 [8192, 512], P('fsdp'), may hold values from -4 to 4
- key_scales: float32 [8192, 2], P('fsdp'), may hold values from 0.0044194176 to 0.027621359
Outputs:
- key_grad: float32 [8192, 512], P(('fsdp', 'dp'))
The draws below stay inside these ranges and needn't reach their ends.
Inputs may be any that keep to these rules, and one draw needn't show every extreme that they name: counts[r] is how many of device r's 4 microbatch slots hold a live microbatch (the first ones).
All inputs are finite; a program needn't handle non-finite values.
Results may differ from the reference program's by a relative error of at most 0.039.
Values may be sent and summed in bfloat16 or wider, within the bound.
A program may use at most 128 MiB of HBM per device.

```python
import math
import jax
import jax.numpy as jnp
from jax import lax

D = 8192
HD = 128
BLOCK = 256
MB_MAX = 4
QH = 32
KW = 512
TOK = 128
TOKENS = 65536
N_DP = 32
N_FSDP = 16
DEVICES = 512


def plant(array, key, low, top_value):
    shape = array.shape
    place = [jax.random.randint(jax.random.fold_in(key, axis), (), 0, shape[axis]) for axis in range(len(shape))]
    array = array.at[tuple(place)].set(low)
    longest = shape.index(max(shape))
    place[longest] = (place[longest] + 1) % shape[longest]
    return array.at[tuple(place)].set(top_value)


def with_spikes(result, rng, source, target, blocks, factor):
    owner, partner = [(jnp.arange(result.shape[dim]) // (result.shape[dim] // blocks)).reshape([-1 if axis == dim else 1 for axis in range(result.ndim)]) for dim in (source, target)]
    chosen = jax.random.permutation(rng, blocks)[partner]
    strong = (owner == chosen) | (owner == (partner + blocks // 2) % blocks)
    return jnp.where(strong, factor * result, result)


def levels(stream_key, dims, split, low, top_value):
    def one(dim, shards_of):
        heights = jax.random.uniform(jax.random.fold_in(jax.random.fold_in(stream_key, 6), dim), (shards_of,), jnp.float32, low / len(split), top_value / len(split))
        return jnp.repeat(jnp.exp(heights), dims[dim] // shards_of).reshape((-1,) + (1,) * (len(dims) - dim - 1))

    loudness = one(*split[0])
    for cut in split[1:]:
        loudness = loudness * one(*cut)
    return loudness


def centred(rng, dims, deviation, bound, cuts=(), held_as=jnp.bfloat16):
    values = jax.random.normal(rng, dims, jnp.float32) * deviation
    if len(cuts) > 0:
        values = levels(rng, dims, cuts, -0.22, 0.18) * values
    return jnp.clip(values, min=-bound, max=bound).astype(held_as)


def bell_draw_with(stream_key, extent, spread, limit, pieces, heavy, held_as=jnp.bfloat16):
    entries = spread * jax.random.normal(stream_key, extent, jnp.float32)
    if pieces:
        entries = entries * levels(stream_key, extent, pieces, -0.22, 0.18)
    return jnp.clip(with_spikes(entries, jax.random.fold_in(stream_key, 3), *heavy), -limit, limit).astype(held_as)


def setup_inputs(seed: int = 0) -> dict:
    splits = jax.random.split(jax.random.key(seed), 8)
    return {
        "counts": plant(jax.random.randint(splits[0], (DEVICES,), 1, MB_MAX + 1), jax.random.fold_in(splits[0], 1), 1, MB_MAX).astype(jnp.int32),
        "tokens": bell_draw_with(splits[1], (TOKENS, D), 1.0, 24.0, ((0, 512),), (0, 1, 512, 6.0)),
        "queries": centred(splits[2], (TOKENS, QH * HD), 1.0, 6.0, ((0, 512),)),
        "values": centred(splits[3], (TOKENS, KW), 1.0, 6.0, ((0, 512),)),
        "out_grad": centred(splits[4], (TOKENS, QH * HD), 1.0, 6.0, ((0, 512),)),
        "key_codes": centred(splits[5], (D, KW), 1.0, 4.0, ((0, 16),)),
        "key_scales": jnp.clip(jnp.exp(math.log(0.027621359) - 1.8325814 * jax.random.uniform(splits[6], (D, KW // BLOCK), jnp.float32) ** levels(splits[6], (D, KW // BLOCK), ((0, 16),), -0.2, 0.2)), 0.0044194176, 0.027621359),
    }


def dequantize(code_rows, scales):
    row_count = code_rows.shape[0]
    blocks = scales.shape[1]
    widened = code_rows.astype(jnp.float32).reshape(row_count, blocks, -1) * scales[:, :, None]
    return widened.reshape(row_count, -1).astype(jnp.bfloat16)

def key_delta_rows(queries, key_rows, values, out_grad, live_count):
    slot_count = MB_MAX
    length = queries.shape[0] // slot_count
    kv_heads = key_rows.shape[1] // HD
    group_size = queries.shape[1] // key_rows.shape[1]
    inverse = 1.0 / math.sqrt(HD)
    query_f = queries.astype(jnp.float32).reshape(slot_count, length, kv_heads, group_size, HD)
    key_f = key_rows.astype(jnp.float32).reshape(slot_count, length, kv_heads, HD)
    value_f = values.astype(jnp.float32).reshape(slot_count, length, kv_heads, HD)
    grad_f = out_grad.astype(jnp.float32).reshape(slot_count, length, kv_heads, group_size, HD)
    scores = jnp.einsum('mqhgd,mkhd->mhgqk', query_f, key_f) * inverse
    position = jnp.arange(length)
    causal = (position[:, None] >= position[None, :]).astype(jnp.float32)
    attention = jnp.exp(scores) * causal
    attention = attention / lax.optimization_barrier(jnp.sum(attention, axis=-1, keepdims=True))
    prob_grad = jnp.einsum('mqhgd,mkhd->mhgqk', grad_f, value_f)
    row_delta = lax.optimization_barrier(jnp.sum(attention * prob_grad, axis=-1, keepdims=True))
    dscore = (attention * (prob_grad - row_delta)).astype(jnp.bfloat16)
    key_grad = jnp.einsum('mhgqk,mqhgd->mkhd', dscore.astype(jnp.float32), query_f) * inverse
    live_slot = (jnp.arange(slot_count) < live_count).astype(jnp.float32)
    key_grad = key_grad * live_slot[:, None, None, None]
    return key_grad.reshape(slot_count * length, kv_heads * HD).astype(jnp.bfloat16)

def reference(counts, tokens, queries, values, out_grad, key_codes, key_scales):
    devices = N_DP * N_FSDP
    key_weight = dequantize(key_codes, key_scales)
    key_rows = jnp.dot(tokens, key_weight, preferred_element_type=jnp.float32).astype(jnp.bfloat16)

    def one_device(inputs):
        return key_delta_rows(inputs[0], inputs[1], inputs[2], inputs[3], inputs[4])
    deltas = lax.map(one_device, (queries.reshape(devices, TOK, -1), key_rows.reshape(devices, TOK, -1), values.reshape(devices, TOK, -1), out_grad.reshape(devices, TOK, -1), counts))
    token_groups = tokens.reshape(N_DP, N_FSDP * TOK, D)
    delta_groups = deltas.reshape(N_DP, N_FSDP * TOK, KW)

    def add_group(running, group_pair):
        section_sum = lax.dot_general(group_pair[0], group_pair[1], (((0,), (0,)), ((), ())), preferred_element_type=jnp.float32)
        return (running + section_sum, None)
    running, unused = lax.scan(add_group, jnp.zeros((D, KW), jnp.float32), (token_groups, delta_groups))
    factor = 1.0 / math.sqrt(devices * TOK)
    return running * factor
```

```python
import functools
import math

import jax
import jax.numpy as jnp
from jax import lax
from jax.experimental import pallas as pl
from jax.experimental.pallas import tpu as pltpu
from jax.sharding import PartitionSpec as P

MESH = pl.DeviceIdType.MESH
F32 = jnp.float32
BF16 = jnp.bfloat16
HD = 128
RING = 4
TOK = 128
MB = 32
SHARD = 512
HALF = 256
QUARTER = 128
GROUP = 8
QW = 2048
OFFSETS = (2, 1, -1, 0)


def kernel(
    nz,
    counts,
    tokens,
    queries,
    values,
    out_grad,
    codes,
    scales,
    out,
    codes_v,
    scales_v,
    cnt,
    tok,
    tok_t,
    q2,
    v2,
    og2,
    wbuf,
    acc,
    keys,
    delta,
    part,
    rs_send,
    rs_recv,
    z_send,
    z_recv,
    swap_send,
    swap_recv,
    load_sem,
    core_send,
    core_recv,
    ag_send,
    ag_recv,
    r_send,
    r_recv,
    zs_sem,
    zr_sem,
):
    dp = lax.axis_index("dp")
    f = lax.axis_index("fsdp")
    x, y = f // RING, f % RING
    z, core = dp // 2, dp % 2
    other = 1 - core
    partner = (2 * z + other, f)

    def wrap(v):
        return (v + 2 * RING) % RING

    def chip(dx, dy):
        return (dp, wrap(x + dx) * RING + wrap(y + dy))

    def along(half, axis, step):
        if half == axis:
            return chip(step, 0)
        return chip(0, step)

    def block(half, d1, d2):
        dx = d1 * (1 - half) + d2 * half
        dy = d2 * (1 - half) + d1 * half
        return wrap(x + dx) * RING + wrap(y + dy)

    def z_peer(i):
        return (((z + i) % nz) * 2 + core, f)

    mine = pl.ds(pl.multiple_of(core * HALF, HALF), HALF)
    theirs = pl.ds(pl.multiple_of(other * HALF, HALF), HALF)
    mine_q = pl.ds(pl.multiple_of(core * QW, QW), QW)
    theirs_q = pl.ds(pl.multiple_of(other * QW, QW), QW)
    low, high = pl.ds(0, TOK), pl.ds(TOK, TOK)
    loads = [
        pltpu.make_async_copy(src, dst, load_sem.at[i])
        for i, (src, dst) in enumerate(
            [
                (codes.at[:, mine], codes_v),
                (scales, scales_v),
                (tokens, tok.at[low]),
                (queries.at[:, mine_q], q2.at[low]),
                (values.at[:, mine], v2.at[low]),
                (out_grad.at[:, mine_q], og2.at[low]),
            ]
        )
    ]
    for load in loads:
        load.start()
    cnt[0] = jnp.full((8, 128), counts[0], jnp.int32)

    barrier = pltpu.get_barrier_semaphore()
    neighbours = [partner, chip(1, 0), chip(-1, 0), chip(0, 1), chip(0, -1)]
    for device in neighbours:
        pl.semaphore_signal(barrier, inc=1, device_id=device, device_id_type=MESH)

    def greet(i, carry):
        pl.semaphore_signal(barrier, inc=1, device_id=z_peer(i), device_id_type=MESH)
        return carry

    lax.fori_loop(1, nz, greet, 0)

    loads[0].wait()
    loads[1].wait()
    scale = jnp.where(core == 0, scales_v[:, 0:1], scales_v[:, 1:2])
    weight = (codes_v[...].astype(F32) * scale).astype(BF16)
    wbuf[f, 0] = weight[:HALF]
    wbuf[f, 1] = weight[HALF:]

    pl.semaphore_wait(barrier, len(neighbours) + nz - 1)

    def remote(src, dst, send, recv, device):
        return pltpu.make_async_remote_copy(
            src_ref=src,
            dst_ref=dst,
            send_sem=send,
            recv_sem=recv,
            device_id=device,
            device_id_type=MESH,
        )

    upper, lower = pl.ds(0, QUARTER), pl.ds(QUARTER, QUARTER)
    whole = pl.ds(0, HALF)
    ag_sent = []

    def ag_copy(half, index, o, rows, axis, step):
        k = half * 20 + index
        ref = wbuf.at[o, half, rows]
        return remote(ref, ref, ag_send.at[k], ag_recv.at[k], along(half, axis, step))

    def ag_start(*args):
        copy = ag_copy(*args)
        copy.start()
        ag_sent.append(copy)

    def ag_wait(half, index, rows):
        ag_copy(half, index, f, rows, 0, 1).wait_recv()

    FIRST = (0, -1, 1, 2)

    def both(half, index, d1, d2, axis):
        ag_start(half, index, block(half, d1, d2), whole, axis, 1)
        ag_start(half, index + 1, block(half, d1, d2), whole, axis, -1)

    for half in (0, 1):
        both(half, 0, 0, 0, 0)
    for half in (0, 1):
        both(half, 4, 0, 0, 1)

    core_copies = [
        remote(src, dst, core_send.at[i], core_recv.at[i], partner)
        for i, (src, dst) in enumerate(
            [
                (tokens, tok.at[high]),
                (queries.at[:, theirs_q], q2.at[high]),
                (out_grad.at[:, theirs_q], og2.at[high]),
                (values.at[:, theirs], v2.at[high]),
                (cnt.at[0], cnt.at[1]),
            ]
        )
    ]
    for copy in core_copies:
        copy.start()

    def project(d1, d2):
        def body(half, carry):
            o = block(half, d1, d2)
            columns = pl.ds(pl.multiple_of(o * SHARD + half * HALF, HALF), HALF)
            acc[...] += jnp.dot(tok[:, columns], wbuf[o, half], preferred_element_type=F32)
            return carry

        lax.fori_loop(0, 2, body, 0)

    def transpose(first, last):
        def body(k, carry):
            piece = pl.ds(pl.multiple_of(k * HALF, HALF), HALF)
            tok_t[piece, :] = tok[:, piece].T
            return carry

        lax.fori_loop(first, last, body, 0)

    def first_pass():
        for half in (0, 1):
            ag_wait(half, 0, whole)
            ag_start(half, 2, block(half, -1, 0), upper, 0, 1)
            both(half, 8, -1, 0, 1)
            ag_wait(half, 1, whole)
            ag_start(half, 3, block(half, 1, 0), lower, 0, -1)
            both(half, 12, 1, 0, 1)

    def second_pass(j):
        for half in (0, 1):
            base = 4 + 4 * j
            ag_wait(half, base, whole)
            ag_start(half, base + 2, block(half, FIRST[j], -1), upper, 1, 1)
            ag_wait(half, base + 1, whole)
            ag_start(half, base + 3, block(half, FIRST[j], 1), lower, 1, -1)

    def second_end(j):
        for half in (0, 1):
            ag_wait(half, 4 + 4 * j + 2, upper)
            ag_wait(half, 4 + 4 * j + 3, lower)

    acc[...] = jnp.zeros_like(acc)
    first_pass()
    loads[2].wait()
    core_copies[0].wait_recv()
    project(0, 0)
    project(-1, 0)
    project(1, 0)
    transpose(0, 8)
    second_pass(0)
    project(0, -1)
    project(0, 1)
    for half in (0, 1):
        ag_wait(half, 2, upper)
        ag_wait(half, 3, lower)
        both(half, 16, 2, 0, 1)
    project(2, 0)
    transpose(8, 16)
    second_pass(1)
    project(-1, -1)
    project(-1, 1)
    second_end(0)
    project(0, 2)
    transpose(16, 24)
    second_pass(2)
    project(1, -1)
    project(1, 1)
    second_end(1)
    project(-1, 2)
    transpose(24, 32)
    second_pass(3)
    second_end(2)
    project(1, 2)
    project(2, -1)
    project(2, 1)
    second_end(3)
    project(2, 2)
    keys[...] = acc[...].astype(BF16)

    for load in loads[3:]:
        load.wait()
    for copy in core_copies[1:]:
        copy.wait_recv()
    inverse = 1.0 / math.sqrt(HD)
    key_at = lax.broadcasted_iota(jnp.int32, (MB, GROUP * MB), 0)
    query_at = lax.broadcasted_iota(jnp.int32, (MB, GROUP * MB), 1) % MB
    seen = key_at <= query_at
    contract_last = (((1,), (1,)), ((), ()))

    def microbatch(m, carry):
        rows = pl.ds(pl.multiple_of(m * MB, MB), MB)
        live = (m % 4) < cnt[m // 4][0:1]
        for head in range(2):
            columns = pl.ds(head * HD, HD)
            start = head * GROUP * HD
            query = jnp.concatenate(
                [q2[rows, pl.ds(start + g * HD, HD)] for g in range(GROUP)], axis=0
            )
            grad = jnp.concatenate(
                [og2[rows, pl.ds(start + g * HD, HD)] for g in range(GROUP)], axis=0
            )
            scores = lax.dot_general(
                keys[rows, columns], query, contract_last, preferred_element_type=F32
            )
            weights = jnp.where(seen, jnp.exp(scores * inverse), 0.0)
            probs = weights / jnp.sum(weights, axis=0, keepdims=True)
            prob_grad = lax.dot_general(
                v2[rows, columns], grad, contract_last, preferred_element_type=F32
            )
            row_delta = jnp.sum(probs * prob_grad, axis=0, keepdims=True)
            dscore = (probs * (prob_grad - row_delta)).astype(BF16)
            key_grad = jnp.dot(dscore, query, preferred_element_type=F32) * inverse
            delta[rows, columns] = jnp.where(live, key_grad, 0.0).astype(BF16)
        return carry

    lax.fori_loop(0, 2 * TOK // MB, microbatch, 0)

    rs_sent = []

    def rs_copy(half, n, index):
        k = (half * 5 + n) * 6 + index
        axis = 0 if n < 4 else 1
        return remote(
            rs_send.at[half, n, index],
            rs_recv.at[half, n, index],
            r_send.at[k],
            r_recv.at[k],
            along(half, axis, 1 if index % 2 == 0 else -1),
        )

    def rs_start(half, n, index, value):
        rs_send[half, n, index] = value.astype(BF16)
        copy = rs_copy(half, n, index)
        copy.start()
        rs_sent.append(copy)

    def rs_take(half, n, index):
        rs_copy(half, n, index).wait_recv()
        return rs_recv[half, n, index].astype(F32)

    def begin(n):
        def body(i, carry):
            half = i % 2
            d = i // 2
            d1 = (d == 0) * 2 + (d == 1) * 1 - (d == 2) * 1
            o = block(half, d1, OFFSETS[n])
            rows = pl.ds(pl.multiple_of(o * SHARD + half * HALF, HALF), HALF)
            part[n % 2, half, d] = jnp.dot(tok_t[rows, :], delta[...], preferred_element_type=F32)
            return carry

        lax.fori_loop(0, 8, body, 0)
        for half in (0, 1):
            rs_start(half, n, 0, part[n % 2, half, 0, :QUARTER])
            rs_start(half, n, 1, part[n % 2, half, 0, QUARTER:])
            rs_start(half, n, 2, part[n % 2, half, 1, QUARTER:])
            rs_start(half, n, 3, part[n % 2, half, 2, :QUARTER])

    def combine(n):
        for half in (0, 1):
            rs_start(half, n, 4, part[n % 2, half, 1, :QUARTER] + rs_take(half, n, 0))
            rs_start(half, n, 5, part[n % 2, half, 2, QUARTER:] + rs_take(half, n, 1))

    def finish(n):
        for half in (0, 1):
            top = part[n % 2, half, 3, :QUARTER] + rs_take(half, n, 3) + rs_take(half, n, 4)
            bottom = part[n % 2, half, 3, QUARTER:] + rs_take(half, n, 2) + rs_take(half, n, 5)
            if n == 0:
                rs_start(half, 4, 0, top)
                rs_start(half, 4, 1, bottom)
            if n == 1:
                rs_start(half, 4, 2, bottom)
                rs_start(half, 4, 4, top + rs_take(half, 4, 0))
            if n == 2:
                rs_start(half, 4, 3, top)
                rs_start(half, 4, 5, bottom + rs_take(half, 4, 1))
            if n == 3:
                top = top + rs_take(half, 4, 3) + rs_take(half, 4, 4)
                bottom = bottom + rs_take(half, 4, 2) + rs_take(half, 4, 5)
                z_send[half * HALF : half * HALF + QUARTER] = top.astype(BF16)
                z_send[half * HALF + QUARTER : (half + 1) * HALF] = bottom.astype(BF16)

    begin(0)
    for n in range(4):
        if n < 3:
            begin(n + 1)
        combine(n)
        finish(n)

    width = SHARD // nz

    def z_rows(i):
        return pl.ds(pl.multiple_of(((z + i) % nz) * width, width), width)

    def z_copy(i):
        return remote(z_send.at[z_rows(i)], z_recv.at[i], zs_sem.at[i], zr_sem.at[i], z_peer(i))

    def z_start(i, carry):
        z_copy(i).start()
        return carry

    def z_add(i, carry):
        z_copy(i).wait_recv()
        return carry + z_recv[i].astype(F32)

    lax.fori_loop(1, nz, z_start, 0)
    total = z_send[z_rows(0), :].astype(F32)
    total = lax.fori_loop(1, nz, z_add, total)
    total = total * (1.0 / math.sqrt(nz * 2 * RING * RING * TOK))

    per = width // 2
    top, bottom = total[:per], total[per:]
    swap_send[...] = jnp.where(core == 0, bottom, top)
    swap = remote(swap_send, swap_recv, core_send.at[5], core_recv.at[5], partner)
    swap.start()
    kept = jnp.where(core == 0, top, bottom)
    swap.wait_recv()
    came = swap_recv[...]
    out[:, :HALF] = jnp.where(core == 0, kept, came)
    out[:, HALF:] = jnp.where(core == 0, came, kept)

    for copy in core_copies:
        copy.wait_send()
    for copy in ag_sent:
        copy.wait_send()
    for copy in rs_sent:
        copy.wait_send()

    def z_sent(i, carry):
        z_copy(i).wait_send()
        return carry

    lax.fori_loop(1, nz, z_sent, 0)
    swap.wait_send()


def local(nz, counts, tokens, queries, values, out_grad, key_codes, key_scales):
    width = SHARD // nz
    return pl.pallas_call(
        functools.partial(kernel, nz),
        out_shape=jax.ShapeDtypeStruct((width // 2, 2 * HALF), F32),
        in_specs=[pl.BlockSpec(memory_space=pltpu.SMEM)]
        + [pl.BlockSpec(memory_space=pl.ANY)] * 6,
        out_specs=pl.BlockSpec(memory_space=pltpu.VMEM),
        scratch_shapes=[
            pltpu.VMEM((SHARD, HALF), BF16),
            pltpu.VMEM((SHARD, 2), F32),
            pltpu.VMEM((2, 8, 128), jnp.int32),
            pltpu.VMEM((2 * TOK, 16 * SHARD), BF16),
            pltpu.VMEM((16 * SHARD, 2 * TOK), BF16),
            pltpu.VMEM((2 * TOK, QW), BF16),
            pltpu.VMEM((2 * TOK, HALF), BF16),
            pltpu.VMEM((2 * TOK, QW), BF16),
            pltpu.VMEM((16, 2, HALF, HALF), BF16),
            pltpu.VMEM((2 * TOK, HALF), F32),
            pltpu.VMEM((2 * TOK, HALF), BF16),
            pltpu.VMEM((2 * TOK, HALF), BF16),
            pltpu.VMEM((2, 2, 4, HALF, HALF), F32),
            pltpu.VMEM((2, 5, 6, QUARTER, HALF), BF16),
            pltpu.VMEM((2, 5, 6, QUARTER, HALF), BF16),
            pltpu.VMEM((SHARD, HALF), BF16),
            pltpu.VMEM((nz, width, HALF), BF16),
            pltpu.VMEM((width // 2, HALF), F32),
            pltpu.VMEM((width // 2, HALF), F32),
            pltpu.SemaphoreType.DMA((6,)),
            pltpu.SemaphoreType.DMA((6,)),
            pltpu.SemaphoreType.DMA((6,)),
            pltpu.SemaphoreType.DMA((40,)),
            pltpu.SemaphoreType.DMA((40,)),
            pltpu.SemaphoreType.DMA((60,)),
            pltpu.SemaphoreType.DMA((60,)),
            pltpu.SemaphoreType.DMA((nz,)),
            pltpu.SemaphoreType.DMA((nz,)),
        ],
        compiler_params=pltpu.CompilerParams(
            collective_id=0,
            has_side_effects=True,
            vmem_limit_bytes=44 * 1024 * 1024,
        ),
        cost_estimate=pl.CostEstimate(
            flops=2_300_000_000, bytes_accessed=6_000_000, transcendentals=140_000
        ),
    )(counts, tokens, queries, values, out_grad, key_codes, key_scales)


def solution(mesh):
    return jax.shard_map(
        functools.partial(local, mesh.shape["dp"] // 2),
        mesh=mesh,
        in_specs=(
            P(("dp", "fsdp")),
            P(("dp", "fsdp"), None),
            P(("dp", "fsdp"), None),
            P(("dp", "fsdp"), None),
            P(("dp", "fsdp"), None),
            P("fsdp", None),
            P("fsdp", None),
        ),
        out_specs=P(("fsdp", "dp"), None),
        check_vma=False,
    )
```

```python
import functools
import math

import jax
import jax.numpy as jnp
from jax import lax
from jax.experimental import pallas as pl
from jax.experimental.pallas import tpu as pltpu
from jax.sharding import PartitionSpec as P

MESH = pl.DeviceIdType.MESH
F32 = jnp.float32
BF16 = jnp.bfloat16
HD = 128
RING = 4
TOK = 128
MB = 32
SHARD = 512
HALF = 256
QUARTER = 128
GROUP = 8
QW = 2048
CHUNKS = 4
WIDE = 4096


def kernel(
    nz,
    counts,
    tokens,
    queries,
    values,
    out_grad,
    codes,
    scales,
    out,
    codes_v,
    scales_v,
    cnt,
    tok,
    tok_t,
    q2,
    v2,
    og2,
    wbuf,
    acc,
    keys,
    d_send,
    d_pair,
    tok_z,
    part,
    rs_send,
    rs_recv,
    z_send,
    z_recv,
    swap_send,
    swap_recv,
    load_sem,
    core_send,
    core_recv,
    ag_send,
    ag_recv,
    r_send,
    r_recv,
    zs_sem,
    zr_sem,
    t_send,
    t_recv,
    f_send,
    f_recv,
    d_ssem,
    d_rsem,
):
    dp = lax.axis_index("dp")
    f = lax.axis_index("fsdp")
    x, y = f // RING, f % RING
    z, core = dp // 2, dp % 2
    other = 1 - core
    partner = (2 * z + other, f)

    def wrap(v):
        return (v + 2 * RING) % RING

    def chip(dx, dy):
        return (dp, wrap(x + dx) * RING + wrap(y + dy))

    def along(half, axis, step):
        if half == axis:
            return chip(step, 0)
        return chip(0, step)

    def block(half, d1, d2):
        dx = d1 * (1 - half) + d2 * half
        dy = d2 * (1 - half) + d1 * half
        return wrap(x + dx) * RING + wrap(y + dy)

    def z_peer(i):
        return (((z + i) % nz) * 2 + core, f)

    parity = z % 2
    pair = (z_peer(nz + 1 - 2 * parity), z_peer(nz - 1 + 2 * parity))

    mine = pl.ds(pl.multiple_of(core * HALF, HALF), HALF)
    theirs = pl.ds(pl.multiple_of(other * HALF, HALF), HALF)
    mine_q = pl.ds(pl.multiple_of(core * QW, QW), QW)
    theirs_q = pl.ds(pl.multiple_of(other * QW, QW), QW)
    low, high = pl.ds(0, TOK), pl.ds(TOK, TOK)
    loads = [
        pltpu.make_async_copy(src, dst, load_sem.at[i])
        for i, (src, dst) in enumerate(
            [
                (codes.at[:, mine], codes_v),
                (scales, scales_v),
                (tokens, tok.at[low]),
                (queries.at[:, mine_q], q2.at[low]),
                (values.at[:, mine], v2.at[low]),
                (out_grad.at[:, mine_q], og2.at[low]),
            ]
        )
    ]
    for load in loads:
        load.start()
    cnt[0] = jnp.full((8, 128), counts[0], jnp.int32)

    barrier = pltpu.get_barrier_semaphore()
    neighbours = [partner, chip(1, 0), chip(-1, 0), chip(0, 1), chip(0, -1)]
    for device in neighbours:
        pl.semaphore_signal(barrier, inc=1, device_id=device, device_id_type=MESH)

    def greet(i, carry):
        pl.semaphore_signal(barrier, inc=1, device_id=z_peer(i), device_id_type=MESH)
        return carry

    lax.fori_loop(1, nz, greet, 0)

    loads[0].wait()
    loads[1].wait()
    scale = jnp.where(core == 0, scales_v[:, 0:1], scales_v[:, 1:2])
    weight = (codes_v[...].astype(F32) * scale).astype(BF16)
    wbuf[f, 0] = weight[:HALF]
    wbuf[f, 1] = weight[HALF:]

    pl.semaphore_wait(barrier, len(neighbours) + nz - 1)

    def remote(src, dst, send, recv, device):
        return pltpu.make_async_remote_copy(
            src_ref=src,
            dst_ref=dst,
            send_sem=send,
            recv_sem=recv,
            device_id=device,
            device_id_type=MESH,
        )

    upper, lower = pl.ds(0, QUARTER), pl.ds(QUARTER, QUARTER)
    whole = pl.ds(0, HALF)
    ag_sent = []

    def ag_copy(half, index, o, rows, axis, step):
        k = half * 20 + index
        ref = wbuf.at[o, half, rows]
        return remote(ref, ref, ag_send.at[k], ag_recv.at[k], along(half, axis, step))

    def ag_start(*args):
        copy = ag_copy(*args)
        copy.start()
        ag_sent.append(copy)

    def ag_wait(half, index, rows):
        ag_copy(half, index, f, rows, 0, 1).wait_recv()

    FIRST = (0, -1, 1, 2)

    def both(half, index, d1, d2, axis):
        ag_start(half, index, block(half, d1, d2), whole, axis, 1)
        ag_start(half, index + 1, block(half, d1, d2), whole, axis, -1)

    for half in (0, 1):
        both(half, 0, 0, 0, 0)
    for half in (0, 1):
        both(half, 4, 0, 0, 1)

    core_copies = [
        remote(src, dst, core_send.at[i], core_recv.at[i], partner)
        for i, (src, dst) in enumerate(
            [
                (tokens, tok.at[high]),
                (queries.at[:, theirs_q], q2.at[high]),
                (out_grad.at[:, theirs_q], og2.at[high]),
                (values.at[:, theirs], v2.at[high]),
                (cnt.at[0], cnt.at[1]),
            ]
        )
    ]
    for copy in core_copies:
        copy.start()

    def swap_copy(k, q):
        i = k * CHUNKS + q
        columns = pl.ds(k * WIDE + q * (WIDE // CHUNKS), WIDE // CHUNKS)
        into = pl.ds(q * (WIDE // CHUNKS), WIDE // CHUNKS)
        return remote(
            tokens.at[:, columns], tok_z.at[k, low, into], t_send.at[i], t_recv.at[i], pair[k]
        )

    def pass_copy(k, q):
        i = k * CHUNKS + q
        into = pl.ds(q * (WIDE // CHUNKS), WIDE // CHUNKS)
        return remote(
            tok_z.at[k, low, into], tok_z.at[k, high, into], f_send.at[i], f_recv.at[i], partner
        )

    for q in range(CHUNKS):
        for k in (0, 1):
            swap_copy(k, q).start()

    def pass_on(q):
        for k in (0, 1):
            swap_copy(k, q).wait_recv()
            pass_copy(k, q).start()

    def transpose_pair(q):
        for k in (0, 1):
            pass_copy(k, q).wait_recv()

        def body(i, carry):
            k = i // 4
            at = q * (WIDE // CHUNKS) + (i % 4) * HALF
            columns = pl.ds(pl.multiple_of(at, HALF), HALF)
            rows = pl.ds(pl.multiple_of(k * WIDE + at, HALF), HALF)
            tok_t[rows, 2 * TOK :] = tok_z[k, :, columns].T
            return carry

        lax.fori_loop(0, 8, body, 0)

    def project(d1, d2):
        def body(half, carry):
            o = block(half, d1, d2)
            columns = pl.ds(pl.multiple_of(o * SHARD + half * HALF, HALF), HALF)
            acc[...] += jnp.dot(tok[:, columns], wbuf[o, half], preferred_element_type=F32)
            return carry

        lax.fori_loop(0, 2, body, 0)

    def transpose(first, last):
        def body(k, carry):
            piece = pl.ds(pl.multiple_of(k * HALF, HALF), HALF)
            tok_t[piece, : 2 * TOK] = tok[:, piece].T
            return carry

        lax.fori_loop(first, last, body, 0)

    def first_pass():
        for half in (0, 1):
            ag_wait(half, 0, whole)
            ag_start(half, 2, block(half, -1, 0), upper, 0, 1)
            both(half, 8, -1, 0, 1)
            ag_wait(half, 1, whole)
            ag_start(half, 3, block(half, 1, 0), lower, 0, -1)
            both(half, 12, 1, 0, 1)

    def second_pass(j):
        for half in (0, 1):
            base = 4 + 4 * j
            ag_wait(half, base, whole)
            ag_start(half, base + 2, block(half, FIRST[j], -1), upper, 1, 1)
            ag_wait(half, base + 1, whole)
            ag_start(half, base + 3, block(half, FIRST[j], 1), lower, 1, -1)

    def second_end(j):
        for half in (0, 1):
            ag_wait(half, 4 + 4 * j + 2, upper)
            ag_wait(half, 4 + 4 * j + 3, lower)

    acc[...] = jnp.zeros_like(acc)
    first_pass()
    loads[2].wait()
    core_copies[0].wait_recv()
    project(0, 0)
    project(-1, 0)
    project(1, 0)
    transpose(0, 8)
    second_pass(0)
    project(0, -1)
    project(0, 1)
    pass_on(0)
    for half in (0, 1):
        ag_wait(half, 2, upper)
        ag_wait(half, 3, lower)
        both(half, 16, 2, 0, 1)
    project(2, 0)
    transpose(8, 16)
    second_pass(1)
    project(-1, -1)
    project(-1, 1)
    second_end(0)
    project(0, 2)
    transpose(16, 24)
    pass_on(1)
    second_pass(2)
    project(1, -1)
    project(1, 1)
    second_end(1)
    project(-1, 2)
    transpose(24, 32)
    transpose_pair(0)
    pass_on(2)
    second_pass(3)
    transpose_pair(1)
    second_end(2)
    project(1, 2)
    project(2, -1)
    project(2, 1)
    second_end(3)
    project(2, 2)
    keys[...] = acc[...].astype(BF16)

    for load in loads[3:]:
        load.wait()
    for copy in core_copies[1:]:
        copy.wait_recv()
    inverse = 1.0 / math.sqrt(HD)
    key_at = lax.broadcasted_iota(jnp.int32, (MB, GROUP * MB), 0)
    query_at = lax.broadcasted_iota(jnp.int32, (MB, GROUP * MB), 1) % MB
    seen = key_at <= query_at
    contract_last = (((1,), (1,)), ((), ()))

    def attend(head, result):
        columns = pl.ds(pl.multiple_of(head * HD, HD), HD)

        def group(ref, rows):
            return jnp.concatenate(
                [
                    ref[rows, pl.ds(pl.multiple_of((head * GROUP + g) * HD, HD), HD)]
                    for g in range(GROUP)
                ],
                axis=0,
            )

        def microbatch(m):
            rows = pl.ds(pl.multiple_of(m * MB, MB), MB)
            live = (m % 4) < cnt[m // 4][0:1]
            query = group(q2, rows)
            scores = lax.dot_general(
                keys[rows, columns], query, contract_last, preferred_element_type=F32
            )
            weights = jnp.where(seen, jnp.exp(scores * inverse), 0.0)
            probs = weights / jnp.sum(weights, axis=0, keepdims=True)
            prob_grad = lax.dot_general(
                v2[rows, columns], group(og2, rows), contract_last, preferred_element_type=F32
            )
            row_delta = jnp.sum(probs * prob_grad, axis=0, keepdims=True)
            dscore = (probs * (prob_grad - row_delta)).astype(BF16)
            key_grad = jnp.dot(dscore, query, preferred_element_type=F32) * inverse
            result[rows, :] = jnp.where(live, key_grad, 0.0).astype(BF16)

        def body(i, carry):
            microbatch(2 * i)
            microbatch(2 * i + 1)
            return carry

        lax.fori_loop(0, TOK // MB, body, 0)

    def delta_copy(k):
        return remote(d_send, d_pair.at[k, pl.ds(2 * TOK, 2 * TOK)], d_ssem.at[k], d_rsem.at[k], pair[k])

    pass_on(3)
    attend(1 - parity, d_send)
    for k in (0, 1):
        delta_copy(k).start()
    transpose_pair(2)
    attend(parity, d_pair.at[0, pl.ds(0, 2 * TOK)])
    d_pair[1, : 2 * TOK] = d_pair[0, : 2 * TOK]
    transpose_pair(3)
    for k in (0, 1):
        delta_copy(k).wait_recv()

    def rs_copy(half, n, index):
        k = (half * 5 + n) * 6 + index
        axis = 1 if isinstance(n, int) and n == 4 else 0
        return remote(
            rs_send.at[half, n, index],
            rs_recv.at[half, n, index],
            r_send.at[k],
            r_recv.at[k],
            along(half, axis, 1 if index % 2 == 0 else -1),
        )

    def rs_start(half, n, index, value):
        rs_send[half, n, index] = value.astype(BF16)
        rs_copy(half, n, index).start()

    def rs_take(half, n, index):
        rs_copy(half, n, index).wait_recv()
        return rs_recv[half, n, index].astype(F32)

    def partial(half, d1, d2):
        o = block(half, d1, d2)
        rows = pl.ds(pl.multiple_of(o * SHARD + half * HALF, HALF), HALF)
        return jnp.dot(tok_t[rows, :], d_pair[o // 8], preferred_element_type=F32)

    def begin(n, carry):
        d2 = jnp.where(n == 3, 0, jnp.where(n == 2, -1, 2 - n))
        for half in (0, 1):
            opposite = partial(half, 2, d2)
            rs_start(half, n, 0, opposite[:QUARTER])
            rs_start(half, n, 1, opposite[QUARTER:])
        for half in (0, 1):
            up = partial(half, 1, d2)
            rs_start(half, n, 2, up[QUARTER:])
            part[n, half, 0] = up[:QUARTER]
            down = partial(half, -1, d2)
            rs_start(half, n, 3, down[:QUARTER])
            part[n, half, 1] = down[QUARTER:]
        for half in (0, 1):
            own = partial(half, 0, d2)
            part[n, half, 2] = own[:QUARTER]
            part[n, half, 3] = own[QUARTER:]
        return carry

    def combine(n):
        for half in (0, 1):
            rs_start(half, n, 4, part[n, half, 0] + rs_take(half, n, 0))
            rs_start(half, n, 5, part[n, half, 1] + rs_take(half, n, 1))

    def finish(n):
        for half in (0, 1):
            top = part[n, half, 2] + rs_take(half, n, 3) + rs_take(half, n, 4)
            bottom = part[n, half, 3] + rs_take(half, n, 2) + rs_take(half, n, 5)
            if n == 0:
                rs_start(half, 4, 0, top)
                rs_start(half, 4, 1, bottom)
            if n == 1:
                rs_start(half, 4, 2, bottom)
                rs_start(half, 4, 4, top + rs_take(half, 4, 0))
            if n == 2:
                rs_start(half, 4, 3, top)
                rs_start(half, 4, 5, bottom + rs_take(half, 4, 1))
            if n == 3:
                top = top + rs_take(half, 4, 3) + rs_take(half, 4, 4)
                bottom = bottom + rs_take(half, 4, 2) + rs_take(half, 4, 5)
                z_send[half * HALF : half * HALF + QUARTER] = top.astype(BF16)
                z_send[half * HALF + QUARTER : (half + 1) * HALF] = bottom.astype(BF16)

    lax.fori_loop(0, 4, begin, 0)
    combine(0)
    combine(1)
    finish(0)
    combine(2)
    finish(1)
    combine(3)
    finish(2)
    finish(3)

    width = SHARD // nz

    def z_rows(i):
        return pl.ds(pl.multiple_of(((z + i) % nz) * width, width), width)

    def z_copy(i):
        return remote(z_send.at[z_rows(i)], z_recv.at[i], zs_sem.at[i], zr_sem.at[i], z_peer(i))

    def z_start(i, carry):
        z_copy(i).start()
        return carry

    def z_take(i):
        z_copy(i).wait_recv()
        return z_recv[i].astype(F32)

    def z_add(i, carry):
        odd, even = carry
        return odd + z_take(2 * i - 1), even + z_take(2 * i)

    lax.fori_loop(1, nz, z_start, 0)
    same = z_send[z_rows(0), :].astype(F32)
    unlike, same = lax.fori_loop(1, nz // 2, z_add, (jnp.zeros_like(same), same))
    unlike = unlike + z_take(nz - 1)
    total = jnp.concatenate(
        [jnp.where(parity == 0, same, unlike), jnp.where(parity == 0, unlike, same)], axis=1
    )
    total = total * (1.0 / math.sqrt(nz * 2 * RING * RING * TOK))

    per = width // 2
    top, bottom = total[:per], total[per:]
    swap_send[...] = jnp.where(core == 0, bottom, top)
    swap = remote(swap_send, swap_recv, core_send.at[5], core_recv.at[5], partner)
    swap.start()
    kept = jnp.where(core == 0, top, bottom)
    swap.wait_recv()
    came = swap_recv[...]
    out[:, :HALF] = jnp.where(core == 0, kept, came)
    out[:, HALF:] = jnp.where(core == 0, came, kept)

    for copy in core_copies:
        copy.wait_send()
    for copy in ag_sent:
        copy.wait_send()
    for k in (0, 1):
        delta_copy(k).wait_send()
        for q in range(CHUNKS):
            swap_copy(k, q).wait_send()
            pass_copy(k, q).wait_send()

    def rs_done(n, carry):
        for half in (0, 1):
            for index in range(6):
                rs_copy(half, n, index).wait_send()
        return carry

    lax.fori_loop(0, 5, rs_done, 0)

    def z_sent(i, carry):
        z_copy(i).wait_send()
        return carry

    lax.fori_loop(1, nz, z_sent, 0)
    swap.wait_send()


def local(nz, counts, tokens, queries, values, out_grad, key_codes, key_scales):
    width = SHARD // nz
    return pl.pallas_call(
        functools.partial(kernel, nz),
        out_shape=jax.ShapeDtypeStruct((width // 2, 2 * HALF), F32),
        in_specs=[pl.BlockSpec(memory_space=pltpu.SMEM)]
        + [pl.BlockSpec(memory_space=pltpu.HBM)] * 6,
        out_specs=pl.BlockSpec(memory_space=pltpu.VMEM),
        scratch_shapes=[
            pltpu.VMEM((SHARD, HALF), BF16),
            pltpu.VMEM((SHARD, 2), F32),
            pltpu.VMEM((2, 8, 128), jnp.int32),
            pltpu.VMEM((2 * TOK, 16 * SHARD), BF16),
            pltpu.VMEM((16 * SHARD, 4 * TOK), BF16),
            pltpu.VMEM((2 * TOK, QW), BF16),
            pltpu.VMEM((2 * TOK, HALF), BF16),
            pltpu.VMEM((2 * TOK, QW), BF16),
            pltpu.VMEM((16, 2, HALF, HALF), BF16),
            pltpu.VMEM((2 * TOK, HALF), F32),
            pltpu.VMEM((2 * TOK, HALF), BF16),
            pltpu.VMEM((2 * TOK, HD), BF16),
            pltpu.VMEM((2, 4 * TOK, HD), BF16),
            pltpu.VMEM((2, 2 * TOK, WIDE), BF16),
            pltpu.VMEM((4, 2, 4, QUARTER, HD), F32),
            pltpu.VMEM((2, 5, 6, QUARTER, HD), BF16),
            pltpu.VMEM((2, 5, 6, QUARTER, HD), BF16),
            pltpu.VMEM((SHARD, HD), BF16),
            pltpu.VMEM((nz, width, HD), BF16),
            pltpu.VMEM((width // 2, HALF), F32),
            pltpu.VMEM((width // 2, HALF), F32),
            pltpu.SemaphoreType.DMA((6,)),
            pltpu.SemaphoreType.DMA((6,)),
            pltpu.SemaphoreType.DMA((6,)),
            pltpu.SemaphoreType.DMA((40,)),
            pltpu.SemaphoreType.DMA((40,)),
            pltpu.SemaphoreType.DMA((60,)),
            pltpu.SemaphoreType.DMA((60,)),
            pltpu.SemaphoreType.DMA((nz,)),
            pltpu.SemaphoreType.DMA((nz,)),
            pltpu.SemaphoreType.DMA((2 * CHUNKS,)),
            pltpu.SemaphoreType.DMA((2 * CHUNKS,)),
            pltpu.SemaphoreType.DMA((2 * CHUNKS,)),
            pltpu.SemaphoreType.DMA((2 * CHUNKS,)),
            pltpu.SemaphoreType.DMA((2,)),
            pltpu.SemaphoreType.DMA((2,)),
        ],
        compiler_params=pltpu.CompilerParams(
            collective_id=0,
            has_side_effects=True,
            vmem_limit_bytes=62 * 1024 * 1024,
        ),
        cost_estimate=pl.CostEstimate(
            flops=2_300_000_000, bytes_accessed=6_000_000, transcendentals=140_000
        ),
    )(counts, tokens, queries, values, out_grad, key_codes, key_scales)


def solution(mesh):
    return jax.shard_map(
        functools.partial(local, mesh.shape["dp"] // 2),
        mesh=mesh,
        in_specs=(
            P(("dp", "fsdp")),
            P(("dp", "fsdp"), None),
            P(("dp", "fsdp"), None),
            P(("dp", "fsdp"), None),
            P(("dp", "fsdp"), None),
            P("fsdp", None),
            P("fsdp", None),
        ),
        out_specs=P(("fsdp", "dp"), None),
        check_vma=False,
    )
```

```python
import functools
import math

import jax
import jax.numpy as jnp
from jax import lax
from jax.experimental import pallas as pl
from jax.experimental.pallas import tpu as pltpu
from jax.sharding import PartitionSpec as P

MESH = pl.DeviceIdType.MESH
F32 = jnp.float32
BF16 = jnp.bfloat16
HD = 128
RING = 4
TOK = 128
MB = 32
SHARD = 512
HALF = 256
QUARTER = 128
GROUP = 8
QW = 2048
OFFSETS = (2, 1, -1, 0)
CHUNKS = 4
WIDE = 4096


def kernel(
    nz,
    counts,
    tokens,
    queries,
    values,
    out_grad,
    codes,
    scales,
    out,
    codes_v,
    scales_v,
    cnt,
    tok,
    tok_t,
    q2,
    v2,
    og2,
    wbuf,
    acc,
    keys,
    d_send,
    d_pair,
    tok_z,
    part,
    rs_send,
    rs_recv,
    z_send,
    z_recv,
    load_sem,
    core_send,
    core_recv,
    ag_send,
    ag_recv,
    r_send,
    r_recv,
    zs_sem,
    zr_sem,
    t_send,
    t_recv,
    f_send,
    f_recv,
    d_ssem,
    d_rsem,
    relay,
):
    dp = lax.axis_index("dp")
    f = lax.axis_index("fsdp")
    x, y = f // RING, f % RING
    z, core = dp // 2, dp % 2
    other = 1 - core
    partner = (2 * z + other, f)

    def wrap(v):
        return (v + 2 * RING) % RING

    def chip(dx, dy):
        return (dp, wrap(x + dx) * RING + wrap(y + dy))

    def along(half, axis, step):
        if half == axis:
            return chip(step, 0)
        return chip(0, step)

    def block(half, d1, d2):
        dx = d1 * (1 - half) + d2 * half
        dy = d2 * (1 - half) + d1 * half
        return wrap(x + dx) * RING + wrap(y + dy)

    def z_peer(i):
        return (((z + i) % nz) * 2 + core, f)

    parity = z % 2
    pair = (z_peer(nz + 1 - 2 * parity), z_peer(nz - 1 + 2 * parity))

    mine = pl.ds(pl.multiple_of(core * HALF, HALF), HALF)
    theirs = pl.ds(pl.multiple_of(other * HALF, HALF), HALF)
    mine_q = pl.ds(pl.multiple_of(core * QW, QW), QW)
    theirs_q = pl.ds(pl.multiple_of(other * QW, QW), QW)
    low, high = pl.ds(0, TOK), pl.ds(TOK, TOK)
    loads = [
        pltpu.make_async_copy(src, dst, load_sem.at[i])
        for i, (src, dst) in enumerate(
            [
                (codes.at[:, mine], codes_v),
                (scales, scales_v),
                (tokens, tok.at[low]),
                (queries.at[:, mine_q], q2.at[low]),
                (values.at[:, mine], v2.at[low]),
                (out_grad.at[:, mine_q], og2.at[low]),
            ]
        )
    ]
    for load in loads:
        load.start()
    cnt[0] = jnp.full((8, 128), counts[0], jnp.int32)

    barrier = pltpu.get_barrier_semaphore()
    neighbours = [partner, chip(1, 0), chip(-1, 0), chip(0, 1), chip(0, -1), *pair]
    for device in neighbours:
        pl.semaphore_signal(barrier, inc=1, device_id=device, device_id_type=MESH)

    loads[0].wait()
    loads[1].wait()
    scale = jnp.where(core == 0, scales_v[0:1], scales_v[1:2])
    scale = jnp.broadcast_to(scale, (HD, SHARD)).T
    left = (codes_v[:, :HD].astype(F32) * scale).astype(BF16)
    right = (codes_v[:, HD:].astype(F32) * scale).astype(BF16)
    for half in (0, 1):
        rows = slice(half * HALF, (half + 1) * HALF)
        wbuf[0, f, half] = jnp.where(parity == 0, right[rows], left[rows])
        wbuf[1, f, half] = jnp.where(parity == 0, left[rows], right[rows])

    pl.semaphore_wait(barrier, len(neighbours))

    def remote(src, dst, send, recv, device):
        return pltpu.make_async_remote_copy(
            src_ref=src,
            dst_ref=dst,
            send_sem=send,
            recv_sem=recv,
            device_id=device,
            device_id_type=MESH,
        )

    upper, lower = pl.ds(0, QUARTER), pl.ds(QUARTER, QUARTER)
    whole = pl.ds(0, HALF)
    ag_sent = []

    def ag_copy(p, half, index, o, rows, axis, step):
        k = (p * 2 + half) * 22 + index
        ref = wbuf.at[p, o, half, rows]
        return remote(ref, ref, ag_send.at[k], ag_recv.at[k], along(half, axis, step))

    def ag_start(*args):
        copy = ag_copy(*args)
        copy.start()
        ag_sent.append(copy)

    def ag_wait(p, half, index, rows):
        ag_copy(p, half, index, f, rows, 0, 1).wait_recv()

    FIRST = (0, -1, 1, 2)

    def both(p, half, index, d1, d2, axis):
        ag_start(p, half, index, block(half, d1, d2), whole, axis, 1)
        ag_start(p, half, index + 1, block(half, d1, d2), whole, axis, -1)

    def gather_start(p, axis):
        for half in (0, 1):
            both(p, half, 4 * axis, 0, 0, axis)

    gather_start(0, 0)
    gather_start(0, 1)
    gather_start(1, 0)
    gather_start(1, 1)

    reach = [1 << r for r in range(nz.bit_length()) if 1 << r < nz // 2]

    def tell(r):
        pl.semaphore_signal(
            relay.at[2 * r], inc=1, device_id=z_peer(reach[r]), device_id_type=MESH
        )
        pl.semaphore_signal(
            relay.at[2 * r + 1], inc=1, device_id=z_peer(nz - reach[r]), device_id_type=MESH
        )

    def hear(r):
        pl.semaphore_wait(relay.at[2 * r], 1)
        pl.semaphore_wait(relay.at[2 * r + 1], 1)

    core_copies = [
        remote(src, dst, core_send.at[i], core_recv.at[i], partner)
        for i, (src, dst) in enumerate(
            [
                (tokens, tok.at[high]),
                (queries.at[:, theirs_q], q2.at[high]),
                (out_grad.at[:, theirs_q], og2.at[high]),
                (values.at[:, theirs], v2.at[high]),
                (cnt.at[0], cnt.at[1]),
            ]
        )
    ]
    for copy in core_copies:
        copy.start()

    def swap_copy(k, q):
        i = k * CHUNKS + q
        columns = pl.ds(k * WIDE + q * (WIDE // CHUNKS), WIDE // CHUNKS)
        into = pl.ds(q * (WIDE // CHUNKS), WIDE // CHUNKS)
        return remote(
            tokens.at[:, columns], tok_z.at[k, low, into], t_send.at[i], t_recv.at[i], pair[k]
        )

    def pass_copy(k, q):
        i = k * CHUNKS + q
        into = pl.ds(q * (WIDE // CHUNKS), WIDE // CHUNKS)
        return remote(
            tok_z.at[k, low, into], tok_z.at[k, high, into], f_send.at[i], f_recv.at[i], partner
        )

    for q in range(CHUNKS):
        for k in (0, 1):
            swap_copy(k, q).start()

    def pass_on(q):
        for k in (0, 1):
            swap_copy(k, q).wait_recv()
            pass_copy(k, q).start()

    def transpose_pair(q):
        for k in (0, 1):
            pass_copy(k, q).wait_recv()

        def body(i, carry):
            k = i // 2
            at = q * (WIDE // CHUNKS) + (i % 2) * SHARD
            columns = pl.ds(pl.multiple_of(at, SHARD), SHARD)
            rows = pl.ds(pl.multiple_of(k * WIDE + at, SHARD), SHARD)
            tok_t[rows, 2 * TOK :] = tok_z[k, :, columns].T
            return carry

        lax.fori_loop(0, 4, body, 0)

    def project(p, *offsets):
        total = acc[p]
        for d1, d2 in offsets:
            for half in (0, 1):
                o = block(half, d1, d2)
                columns = pl.ds(pl.multiple_of(o * SHARD + half * HALF, HALF), HALF)
                total += jnp.dot(tok[:, columns], wbuf[p, o, half], preferred_element_type=F32)
        acc[p] = total

    def transpose(first, last):
        def body(k, carry):
            piece = pl.ds(pl.multiple_of(k * SHARD, SHARD), SHARD)
            tok_t[piece, : 2 * TOK] = tok[:, piece].T
            return carry

        lax.fori_loop(first, last, body, 0)

    def first_pass(p):
        for half in (0, 1):
            ag_wait(p, half, 0, whole)
            ag_start(p, half, 2, block(half, -1, 0), upper, 0, 1)
            ag_wait(p, half, 1, whole)
            ag_start(p, half, 3, block(half, 1, 0), lower, 0, -1)

    def second_start(p):
        for half in (0, 1):
            both(p, half, 8, -1, 0, 1)
            both(p, half, 12, 1, 0, 1)

    def first_end(p):
        for half in (0, 1):
            ag_wait(p, half, 2, upper)
            ag_wait(p, half, 3, lower)
            o = block(half, 2, 0)
            ag_start(p, half, 16, o, upper, 1, 1)
            ag_start(p, half, 17, o, lower, 1, -1)
            ag_start(p, half, 21, o, lower, 1, 1)
            ag_start(p, half, 20, o, upper, 1, -1)

    def second_pass(p, j):
        for half in (0, 1):
            base = 4 + 4 * j
            ag_wait(p, half, base, whole if j < 3 else upper)
            ag_start(p, half, base + 2, block(half, FIRST[j], -1), upper, 1, 1)
            ag_wait(p, half, base + 1, whole if j < 3 else lower)
            ag_start(p, half, base + 3, block(half, FIRST[j], 1), lower, 1, -1)

    def second_end(p, j):
        for half in (0, 1):
            ag_wait(p, half, 4 + 4 * j + 2, upper)
            ag_wait(p, half, 4 + 4 * j + 3, lower)

    def second_rest(p):
        for half in (0, 1):
            ag_wait(p, half, 20, upper)
            ag_wait(p, half, 21, lower)

    inverse = 1.0 / math.sqrt(HD)
    key_at = lax.broadcasted_iota(jnp.int32, (MB, GROUP * MB), 0)
    query_at = lax.broadcasted_iota(jnp.int32, (MB, GROUP * MB), 1) % MB
    seen = key_at <= query_at
    contract_last = (((1,), (1,)), ((), ()))

    def attend(p, first, last, result):
        head = (1 - parity) if p == 0 else parity
        columns = pl.ds(pl.multiple_of(head * HD, HD), HD)

        def group(ref, rows):
            return jnp.concatenate(
                [
                    ref[rows, pl.ds(pl.multiple_of((head * GROUP + g) * HD, HD), HD)]
                    for g in range(GROUP)
                ],
                axis=0,
            )

        def microbatch(m):
            rows = pl.ds(pl.multiple_of(m * MB, MB), MB)
            live = (m % 4) < cnt[m // 4][0:1]
            query = group(q2, rows)
            scores = lax.dot_general(
                keys[p, rows, :], query, contract_last, preferred_element_type=F32
            )
            weights = jnp.where(seen, jnp.exp(scores * inverse), 0.0)
            probs = weights / jnp.sum(weights, axis=0, keepdims=True)
            prob_grad = lax.dot_general(
                v2[rows, columns], group(og2, rows), contract_last, preferred_element_type=F32
            )
            row_delta = jnp.sum(probs * prob_grad, axis=0, keepdims=True)
            dscore = (probs * (prob_grad - row_delta)).astype(BF16)
            key_grad = jnp.dot(dscore, query, preferred_element_type=F32) * inverse
            result[rows, :] = jnp.where(live, key_grad, 0.0).astype(BF16)

        def body(i, carry):
            for m in range(4):
                microbatch(4 * i + m)
            return carry

        lax.fori_loop(first, last, body, 0)

    def delta_copy(k):
        return remote(d_send, d_pair.at[k, pl.ds(2 * TOK, 2 * TOK)], d_ssem.at[k], d_rsem.at[k], pair[k])

    tell(0)
    acc[...] = jnp.zeros_like(acc)
    first_pass(0)
    second_start(0)
    second_pass(0, 0)
    hear(0)
    tell(1)
    loads[2].wait()
    core_copies[0].wait_recv()
    first_pass(1)
    transpose(0, 2)
    second_pass(1, 0)
    transpose(2, 4)
    first_end(0)
    second_start(1)
    project(0, (0, 0), (-1, 0), (1, 0), (0, -1), (0, 1))
    second_pass(0, 1)
    transpose(4, 6)
    second_pass(0, 2)
    hear(1)
    tell(2)
    pass_on(0)
    transpose(6, 8)
    first_end(1)
    project(0, (2, 0), (-1, -1), (-1, 1))
    second_pass(0, 3)
    second_end(0, 0)
    second_end(0, 1)
    project(0, (1, -1), (1, 1), (0, 2), (-1, 2))
    transpose(8, 10)
    pass_on(1)
    second_pass(1, 1)
    second_end(0, 2)
    second_pass(1, 2)
    second_rest(0)
    project(0, (1, 2), (2, -1), (2, 1))
    second_end(0, 3)
    project(0, (2, 2))
    keys[0] = acc[0].astype(BF16)
    for load in loads[3:]:
        load.wait()
    for copy in core_copies[1:]:
        copy.wait_recv()
    attend(0, 0, 1, d_send)
    second_pass(1, 3)
    attend(0, 1, 2, d_send)
    for k in (0, 1):
        delta_copy(k).start()
    pass_on(2)
    project(1, (0, 0), (-1, 0), (1, 0), (0, -1), (0, 1), (2, 0))
    second_end(1, 0)
    second_end(1, 1)
    project(1, (-1, -1), (-1, 1), (1, -1), (1, 1), (0, 2), (-1, 2))
    transpose(10, 16)
    hear(2)
    second_end(1, 2)
    second_rest(1)
    project(1, (1, 2), (2, -1), (2, 1))
    transpose_pair(0)
    transpose_pair(1)
    second_end(1, 3)
    project(1, (2, 2))
    keys[1] = acc[1].astype(BF16)
    pass_on(3)
    attend(1, 0, 1, d_pair.at[0, pl.ds(0, 2 * TOK)])
    transpose_pair(2)
    attend(1, 1, 2, d_pair.at[0, pl.ds(0, 2 * TOK)])
    d_pair[1, : 2 * TOK] = d_pair[0, : 2 * TOK]
    transpose_pair(3)
    for k in (0, 1):
        delta_copy(k).wait_recv()

    def rs_copy(half, n, index):
        k = (half * 5 + n) * 6 + index
        axis = 1 if isinstance(n, int) and n == 4 else 0
        return remote(
            rs_send.at[half, n, index],
            rs_recv.at[half, n, index],
            r_send.at[k],
            r_recv.at[k],
            along(half, axis, 1 if index % 2 == 0 else -1),
        )

    def rs_start(half, n, index, value):
        rs_send[half, n, index] = value.astype(BF16)
        rs_copy(half, n, index).start()

    def rs_take(half, n, index):
        rs_copy(half, n, index).wait_recv()
        return rs_recv[half, n, index].astype(F32)

    def partial(half, d1, d2):
        o = block(half, d1, d2)
        rows = pl.ds(pl.multiple_of(o * SHARD + half * HALF, HALF), HALF)
        return jnp.dot(tok_t[rows, :], d_pair[o // 8], preferred_element_type=F32)

    def begin(n):
        d2 = OFFSETS[n]
        for half in (0, 1):
            opposite = partial(half, 2, d2)
            rs_start(half, n, 0, opposite[:QUARTER])
            rs_start(half, n, 1, opposite[QUARTER:])
        for half in (0, 1):
            up = partial(half, 1, d2)
            rs_start(half, n, 2, up[QUARTER:])
            part[n, half, 0] = up[:QUARTER]
            down = partial(half, -1, d2)
            rs_start(half, n, 3, down[:QUARTER])
            part[n, half, 1] = down[QUARTER:]
        for half in (0, 1):
            own = partial(half, 0, d2)
            part[n, half, 2] = own[:QUARTER]
            part[n, half, 3] = own[QUARTER:]

    def combine(n):
        for half in (0, 1):
            rs_start(half, n, 4, part[n, half, 0] + rs_take(half, n, 0))
            rs_start(half, n, 5, part[n, half, 1] + rs_take(half, n, 1))

    def finish(n):
        for half in (0, 1):
            top = part[n, half, 2] + rs_take(half, n, 3) + rs_take(half, n, 4)
            bottom = part[n, half, 3] + rs_take(half, n, 2) + rs_take(half, n, 5)
            if n == 0:
                rs_start(half, 4, 0, top)
                rs_start(half, 4, 1, bottom)
            if n == 1:
                rs_start(half, 4, 2, bottom)
                part[1, half, 2] = top
            if n == 2:
                rs_start(half, 4, 3, top)
                part[2, half, 3] = bottom
            if n == 3:
                top = top + rs_take(half, 4, 3) + rs_take(half, 4, 4)
                bottom = bottom + rs_take(half, 4, 2) + rs_take(half, 4, 5)
                z_send[half * HALF : half * HALF + QUARTER] = top.astype(BF16)
                z_send[half * HALF + QUARTER : (half + 1) * HALF] = bottom.astype(BF16)

    begin(0)
    begin(1)
    combine(0)
    begin(2)
    combine(1)
    begin(3)
    finish(0)
    combine(2)
    combine(3)
    finish(1)
    finish(2)
    for half in (0, 1):
        rs_start(half, 4, 4, part[1, half, 2] + rs_take(half, 4, 0))
        rs_start(half, 4, 5, part[2, half, 3] + rs_take(half, 4, 1))
    finish(3)

    per = SHARD // (2 * nz)

    def z_copy(i, k):
        to = (z + i) % nz
        its = core if k == 0 else other
        rows = pl.ds(pl.multiple_of((2 * to + its) * per, per), per)
        return remote(
            z_send.at[rows],
            z_recv.at[k, i],
            zs_sem.at[k, i],
            zr_sem.at[k, i],
            (2 * to + its, f),
        )

    def z_start(i, carry):
        away = (i + 1) // 2
        distance = nz // 2 + jnp.where(i % 2 == 0, away, -away)
        z_copy(distance, 0).start()
        z_copy(distance, 1).start()
        return carry

    def z_take(i, k):
        z_copy(i, k).wait_recv()
        return z_recv[k, i].astype(F32)

    def z_add(i, carry):
        return tuple(total + z_take(2 * i + n // 2, n % 2) for n, total in enumerate(carry))

    lax.fori_loop(0, nz - 1, z_start, 0)
    z_copy(0, 1).start()
    rows = pl.ds(pl.multiple_of((2 * z + core) * per, per), per)
    mine_sum = z_send[rows, :].astype(F32)
    sums = (mine_sum, z_take(0, 1), z_take(1, 0), z_take(1, 1))
    sums = lax.fori_loop(1, nz // 2, z_add, sums)
    factor = 1.0 / math.sqrt(nz * 2 * RING * RING * TOK)
    even = [jnp.where(parity == 0, sums[k], sums[2 + k]) * factor for k in (0, 1)]
    odd = [jnp.where(parity == 0, sums[2 + k], sums[k]) * factor for k in (0, 1)]
    out[:, :HD] = jnp.where(core == 0, even[0], even[1])
    out[:, HD : 2 * HD] = jnp.where(core == 0, odd[0], odd[1])
    out[:, 2 * HD : 3 * HD] = jnp.where(core == 0, even[1], even[0])
    out[:, 3 * HD :] = jnp.where(core == 0, odd[1], odd[0])

    for copy in core_copies:
        copy.wait_send()
    for copy in ag_sent:
        copy.wait_send()
    for k in (0, 1):
        delta_copy(k).wait_send()
        for q in range(CHUNKS):
            swap_copy(k, q).wait_send()
            pass_copy(k, q).wait_send()

    def rs_done(n, carry):
        for half in (0, 1):
            for index in range(6):
                rs_copy(half, n, index).wait_send()
        return carry

    lax.fori_loop(0, 5, rs_done, 0)

    def z_sent(i, carry):
        z_copy(i, 0).wait_send()
        z_copy(i, 1).wait_send()
        return carry

    z_copy(0, 1).wait_send()
    lax.fori_loop(1, nz, z_sent, 0)


def local(nz, counts, tokens, queries, values, out_grad, key_codes, key_scales):
    width = SHARD // nz
    return pl.pallas_call(
        functools.partial(kernel, nz),
        out_shape=jax.ShapeDtypeStruct((width // 2, 2 * HALF), F32),
        in_specs=[pl.BlockSpec(memory_space=pltpu.SMEM)]
        + [pl.BlockSpec(memory_space=pltpu.HBM)] * 6,
        out_specs=pl.BlockSpec(memory_space=pltpu.VMEM),
        scratch_shapes=[
            pltpu.VMEM((SHARD, HALF), BF16),
            pltpu.VMEM((2, SHARD), F32),
            pltpu.VMEM((2, 8, 128), jnp.int32),
            pltpu.VMEM((2 * TOK, 16 * SHARD), BF16),
            pltpu.VMEM((16 * SHARD, 4 * TOK), BF16),
            pltpu.VMEM((2 * TOK, QW), BF16),
            pltpu.VMEM((2 * TOK, HALF), BF16),
            pltpu.VMEM((2 * TOK, QW), BF16),
            pltpu.VMEM((2, 16, 2, HALF, HD), BF16),
            pltpu.VMEM((2, 2 * TOK, HD), F32),
            pltpu.VMEM((2, 2 * TOK, HD), BF16),
            pltpu.VMEM((2 * TOK, HD), BF16),
            pltpu.VMEM((2, 4 * TOK, HD), BF16),
            pltpu.VMEM((2, 2 * TOK, WIDE), BF16),
            pltpu.VMEM((4, 2, 4, QUARTER, HD), F32),
            pltpu.VMEM((2, 5, 6, QUARTER, HD), BF16),
            pltpu.VMEM((2, 5, 6, QUARTER, HD), BF16),
            pltpu.VMEM((SHARD, HD), BF16),
            pltpu.VMEM((2, nz, width // 2, HD), BF16),
            pltpu.SemaphoreType.DMA((6,)),
            pltpu.SemaphoreType.DMA((6,)),
            pltpu.SemaphoreType.DMA((6,)),
            pltpu.SemaphoreType.DMA((88,)),
            pltpu.SemaphoreType.DMA((88,)),
            pltpu.SemaphoreType.DMA((60,)),
            pltpu.SemaphoreType.DMA((60,)),
            pltpu.SemaphoreType.DMA((2, nz)),
            pltpu.SemaphoreType.DMA((2, nz)),
            pltpu.SemaphoreType.DMA((2 * CHUNKS,)),
            pltpu.SemaphoreType.DMA((2 * CHUNKS,)),
            pltpu.SemaphoreType.DMA((2 * CHUNKS,)),
            pltpu.SemaphoreType.DMA((2 * CHUNKS,)),
            pltpu.SemaphoreType.DMA((2,)),
            pltpu.SemaphoreType.DMA((2,)),
            pltpu.SemaphoreType.REGULAR((8,)),
        ],
        compiler_params=pltpu.CompilerParams(
            collective_id=0,
            has_side_effects=True,
            vmem_limit_bytes=62 * 1024 * 1024,
        ),
        cost_estimate=pl.CostEstimate(
            flops=2_300_000_000, bytes_accessed=6_000_000, transcendentals=140_000
        ),
    )(counts, tokens, queries, values, out_grad, key_codes, key_scales.T)


def solution(mesh):
    return jax.shard_map(
        functools.partial(local, mesh.shape["dp"] // 2),
        mesh=mesh,
        in_specs=(
            P(("dp", "fsdp")),
            P(("dp", "fsdp"), None),
            P(("dp", "fsdp"), None),
            P(("dp", "fsdp"), None),
            P(("dp", "fsdp"), None),
            P("fsdp", None),
            P("fsdp", None),
        ),
        out_specs=P(("fsdp", "dp"), None),
        check_vma=False,
    )
```

```python
import functools
import math

import jax
import jax.numpy as jnp
from jax import lax
from jax.experimental import pallas as pl
from jax.experimental.pallas import tpu as pltpu
from jax.sharding import PartitionSpec as P

MESH = pl.DeviceIdType.MESH
F32 = jnp.float32
BF16 = jnp.bfloat16
HD = 128
RING = 4
TOK = 128
MB = 32
SHARD = 512
HALF = 256
QUARTER = 128
GROUP = 8
QW = 2048
OFFSETS = (2, 1, -1, 0)
CHUNKS = 4
WIDE = 4096


def kernel(
    nz,
    counts,
    tokens,
    queries,
    values,
    out_grad,
    codes,
    scales,
    out,
    codes_v,
    scales_v,
    cnt,
    tok,
    tok_t,
    q2,
    v2,
    og2,
    wbuf,
    acc,
    keys,
    d_send,
    d_pair,
    tok_z,
    part,
    rs_send,
    rs_recv,
    z_send,
    z_recv,
    load_sem,
    core_send,
    core_recv,
    ag_send,
    ag_recv,
    r_send,
    r_recv,
    zs_sem,
    zr_sem,
    t_send,
    t_recv,
    f_send,
    f_recv,
    d_ssem,
    d_rsem,
    relay,
):
    dp = lax.axis_index("dp")
    f = lax.axis_index("fsdp")
    x, y = f // RING, f % RING
    z, core = dp // 2, dp % 2
    other = 1 - core
    partner = (2 * z + other, f)

    def wrap(v):
        return (v + 2 * RING) % RING

    def chip(dx, dy):
        return (dp, wrap(x + dx) * RING + wrap(y + dy))

    def along(half, axis, step):
        if half == axis:
            return chip(step, 0)
        return chip(0, step)

    def block(half, d1, d2):
        dx = d1 * (1 - half) + d2 * half
        dy = d2 * (1 - half) + d1 * half
        return wrap(x + dx) * RING + wrap(y + dy)

    def z_peer(i):
        return (((z + i) % nz) * 2 + core, f)

    parity = z % 2
    pair = (z_peer(nz + 1 - 2 * parity), z_peer(nz - 1 + 2 * parity))

    barrier = pltpu.get_barrier_semaphore()
    neighbours = [partner, chip(1, 0), chip(-1, 0), chip(0, 1), chip(0, -1), *pair]
    for device in neighbours:
        pl.semaphore_signal(barrier, inc=1, device_id=device, device_id_type=MESH)

    mine = pl.ds(pl.multiple_of(core * HALF, HALF), HALF)
    theirs = pl.ds(pl.multiple_of(other * HALF, HALF), HALF)
    mine_q = pl.ds(pl.multiple_of(core * QW, QW), QW)
    theirs_q = pl.ds(pl.multiple_of(other * QW, QW), QW)
    low, high = pl.ds(0, TOK), pl.ds(TOK, TOK)
    loads = [
        pltpu.make_async_copy(src, dst, load_sem.at[i])
        for i, (src, dst) in enumerate(
            [
                (codes.at[:, mine], codes_v),
                (scales, scales_v),
                (tokens, tok.at[low]),
                (queries.at[:, mine_q], q2.at[low]),
                (values.at[:, mine], v2.at[low]),
                (out_grad.at[:, mine_q], og2.at[low]),
            ]
        )
    ]
    for load in loads[:2]:
        load.start()
    loads[0].wait()
    loads[1].wait()
    scale = jnp.where(core == 0, scales_v[0:1], scales_v[1:2])
    scale = jnp.broadcast_to(scale, (HD, SHARD)).T
    left = (codes_v[:, :HD].astype(F32) * scale).astype(BF16)
    right = (codes_v[:, HD:].astype(F32) * scale).astype(BF16)
    for half in (0, 1):
        rows = slice(half * HALF, (half + 1) * HALF)
        wbuf[0, f, half] = jnp.where(parity == 0, right[rows], left[rows])
        wbuf[1, f, half] = jnp.where(parity == 0, left[rows], right[rows])

    for load in loads[2:]:
        load.start()
    pl.semaphore_wait(barrier, len(neighbours))

    def remote(src, dst, send, recv, device):
        return pltpu.make_async_remote_copy(
            src_ref=src,
            dst_ref=dst,
            send_sem=send,
            recv_sem=recv,
            device_id=device,
            device_id_type=MESH,
        )

    upper, lower = pl.ds(0, QUARTER), pl.ds(QUARTER, QUARTER)
    whole = pl.ds(0, HALF)
    ag_sent = []

    def ag_copy(p, half, index, o, rows, axis, step):
        k = (p * 2 + half) * 22 + index
        ref = wbuf.at[p, o, half, rows]
        return remote(ref, ref, ag_send.at[k], ag_recv.at[k], along(half, axis, step))

    def ag_start(*args):
        copy = ag_copy(*args)
        copy.start()
        ag_sent.append(copy)

    def ag_wait(p, half, index, rows):
        ag_copy(p, half, index, f, rows, 0, 1).wait_recv()

    FIRST = (0, -1, 1, 2)

    def both(p, half, index, d1, d2, axis):
        ag_start(p, half, index, block(half, d1, d2), whole, axis, 1)
        ag_start(p, half, index + 1, block(half, d1, d2), whole, axis, -1)

    def gather_start(p, axis):
        for half in (0, 1):
            both(p, half, 4 * axis, 0, 0, axis)

    gather_start(0, 0)
    gather_start(0, 1)
    def swap_copy(k, q):
        i = k * CHUNKS + q
        columns = pl.ds(k * WIDE + q * (WIDE // CHUNKS), WIDE // CHUNKS)
        into = pl.ds(q * (WIDE // CHUNKS), WIDE // CHUNKS)
        return remote(
            tokens.at[:, columns], tok_z.at[k, low, into], t_send.at[i], t_recv.at[i], pair[k]
        )

    for q in range(CHUNKS):
        for k in (0, 1):
            swap_copy(k, q).start()

    gather_start(1, 0)
    gather_start(1, 1)

    reach = [1 << r for r in range(nz.bit_length()) if 1 << r < nz // 2]

    def tell(r):
        pl.semaphore_signal(
            relay.at[2 * r], inc=1, device_id=z_peer(reach[r]), device_id_type=MESH
        )
        pl.semaphore_signal(
            relay.at[2 * r + 1], inc=1, device_id=z_peer(nz - reach[r]), device_id_type=MESH
        )

    def hear(r):
        pl.semaphore_wait(relay.at[2 * r], 1)
        pl.semaphore_wait(relay.at[2 * r + 1], 1)

    core_copies = [
        remote(src, dst, core_send.at[i], core_recv.at[i], partner)
        for i, (src, dst) in enumerate(
            [
                (tokens, tok.at[high]),
                (queries.at[:, theirs_q], q2.at[high]),
                (out_grad.at[:, theirs_q], og2.at[high]),
                (values.at[:, theirs], v2.at[high]),
                (cnt.at[0], cnt.at[1]),
            ]
        )
    ]
    for copy in core_copies[:4]:
        copy.start()

    def pass_copy(k, q):
        i = k * CHUNKS + q
        into = pl.ds(q * (WIDE // CHUNKS), WIDE // CHUNKS)
        return remote(
            tok_z.at[k, low, into], tok_z.at[k, high, into], f_send.at[i], f_recv.at[i], partner
        )

    def pass_on(q):
        for k in (0, 1):
            swap_copy(k, q).wait_recv()
            pass_copy(k, q).start()

    def transpose_pair(q):
        for k in (0, 1):
            pass_copy(k, q).wait_recv()

        def body(i, carry):
            k = i // 2
            at = q * (WIDE // CHUNKS) + (i % 2) * SHARD
            columns = pl.ds(pl.multiple_of(at, SHARD), SHARD)
            rows = pl.ds(pl.multiple_of(k * WIDE + at, SHARD), SHARD)
            tok_t[rows, 2 * TOK :] = tok_z[k, :, columns].T
            return carry

        lax.fori_loop(0, 4, body, 0)

    def project(p, *offsets):
        total = acc[p]
        for d1, d2 in offsets:
            for half in (0, 1):
                o = block(half, d1, d2)
                columns = pl.ds(pl.multiple_of(o * SHARD + half * HALF, HALF), HALF)
                total += jnp.dot(tok[:, columns], wbuf[p, o, half], preferred_element_type=F32)
        acc[p] = total

    def transpose(first, last):
        def body(k, carry):
            piece = pl.ds(pl.multiple_of(k * SHARD, SHARD), SHARD)
            tok_t[piece, : 2 * TOK] = tok[:, piece].T
            return carry

        lax.fori_loop(first, last, body, 0)

    def first_pass(p):
        for half in (0, 1):
            ag_wait(p, half, 0, whole)
            ag_start(p, half, 2, block(half, -1, 0), upper, 0, 1)
            ag_wait(p, half, 1, whole)
            ag_start(p, half, 3, block(half, 1, 0), lower, 0, -1)

    def second_start(p):
        for half in (0, 1):
            both(p, half, 8, -1, 0, 1)
            both(p, half, 12, 1, 0, 1)

    def first_end(p):
        for half in (0, 1):
            ag_wait(p, half, 2, upper)
            ag_wait(p, half, 3, lower)
            o = block(half, 2, 0)
            ag_start(p, half, 16, o, upper, 1, 1)
            ag_start(p, half, 17, o, lower, 1, -1)
            ag_start(p, half, 21, o, lower, 1, 1)
            ag_start(p, half, 20, o, upper, 1, -1)

    def second_pass(p, j):
        for half in (0, 1):
            base = 4 + 4 * j
            ag_wait(p, half, base, whole if j < 3 else upper)
            ag_start(p, half, base + 2, block(half, FIRST[j], -1), upper, 1, 1)
            ag_wait(p, half, base + 1, whole if j < 3 else lower)
            ag_start(p, half, base + 3, block(half, FIRST[j], 1), lower, 1, -1)

    def second_end(p, j):
        for half in (0, 1):
            ag_wait(p, half, 4 + 4 * j + 2, upper)
            ag_wait(p, half, 4 + 4 * j + 3, lower)

    def second_rest(p):
        for half in (0, 1):
            ag_wait(p, half, 20, upper)
            ag_wait(p, half, 21, lower)

    inverse = 1.0 / math.sqrt(HD)
    key_at = lax.broadcasted_iota(jnp.int32, (MB, GROUP * MB), 0)
    query_at = lax.broadcasted_iota(jnp.int32, (MB, GROUP * MB), 1) % MB
    seen = key_at <= query_at
    contract_last = (((1,), (1,)), ((), ()))

    def attend(p, first, last, result):
        head = (1 - parity) if p == 0 else parity
        columns = pl.ds(pl.multiple_of(head * HD, HD), HD)

        def group(ref, rows):
            return jnp.concatenate(
                [
                    ref[rows, pl.ds(pl.multiple_of((head * GROUP + g) * HD, HD), HD)]
                    for g in range(GROUP)
                ],
                axis=0,
            )

        def microbatch(m):
            rows = pl.ds(pl.multiple_of(m * MB, MB), MB)
            live = (m % 4) < cnt[m // 4][0:1]
            query = group(q2, rows)
            scores = lax.dot_general(
                keys[p, rows, :], query, contract_last, preferred_element_type=F32
            )
            weights = jnp.where(seen, jnp.exp(scores * inverse), 0.0)
            probs = weights / jnp.sum(weights, axis=0, keepdims=True)
            prob_grad = lax.dot_general(
                v2[rows, columns], group(og2, rows), contract_last, preferred_element_type=F32
            )
            row_delta = jnp.sum(probs * prob_grad, axis=0, keepdims=True)
            dscore = (probs * (prob_grad - row_delta)).astype(BF16)
            key_grad = jnp.dot(dscore, query, preferred_element_type=F32) * inverse
            result[rows, :] = jnp.where(live, key_grad, 0.0).astype(BF16)

        def body(i, carry):
            for m in range(4):
                microbatch(4 * i + m)
            return carry

        lax.fori_loop(first, last, body, 0)

    def delta_copy(k):
        return remote(d_send, d_pair.at[k, pl.ds(2 * TOK, 2 * TOK)], d_ssem.at[k], d_rsem.at[k], pair[k])

    tell(0)
    cnt[0] = jnp.full((8, 128), counts[0], jnp.int32)
    core_copies[4].start()
    acc[...] = jnp.zeros_like(acc)
    first_pass(0)
    second_start(0)
    second_pass(0, 0)
    hear(0)
    tell(1)
    loads[2].wait()
    core_copies[0].wait_recv()
    first_pass(1)
    transpose(0, 2)
    second_pass(1, 0)
    transpose(2, 4)
    first_end(0)
    second_start(1)
    project(0, (0, 0), (-1, 0), (1, 0), (0, -1), (0, 1))
    second_pass(0, 1)
    transpose(4, 6)
    second_pass(0, 2)
    hear(1)
    tell(2)
    pass_on(0)
    transpose(6, 8)
    first_end(1)
    project(0, (2, 0), (-1, -1), (-1, 1))
    second_pass(0, 3)
    second_end(0, 0)
    second_end(0, 1)
    project(0, (1, -1), (1, 1), (0, 2), (-1, 2))
    transpose(8, 10)
    pass_on(1)
    second_pass(1, 1)
    second_end(0, 2)
    second_pass(1, 2)
    second_rest(0)
    project(0, (1, 2), (2, -1), (2, 1))
    second_end(0, 3)
    project(0, (2, 2))
    keys[0] = acc[0].astype(BF16)
    for load in loads[3:]:
        load.wait()
    for copy in core_copies[1:]:
        copy.wait_recv()
    attend(0, 0, 1, d_send)
    second_pass(1, 3)
    attend(0, 1, 2, d_send)
    for k in (0, 1):
        delta_copy(k).start()
    pass_on(2)
    project(1, (0, 0), (-1, 0), (1, 0), (0, -1), (0, 1), (2, 0))
    second_end(1, 0)
    second_end(1, 1)
    project(1, (-1, -1), (-1, 1), (1, -1), (1, 1), (0, 2), (-1, 2))
    transpose(10, 16)
    hear(2)
    second_end(1, 2)
    second_rest(1)
    project(1, (1, 2), (2, -1), (2, 1))
    transpose_pair(0)
    transpose_pair(1)
    pass_on(3)
    transpose_pair(2)
    second_end(1, 3)
    project(1, (2, 2))
    keys[1] = acc[1].astype(BF16)
    attend(1, 0, 2, d_pair.at[0, pl.ds(0, 2 * TOK)])
    d_pair[1, : 2 * TOK] = d_pair[0, : 2 * TOK]
    transpose_pair(3)
    for k in (0, 1):
        delta_copy(k).wait_recv()

    def rs_copy(half, n, index):
        k = (half * 5 + n) * 6 + index
        axis = 1 if isinstance(n, int) and n == 4 else 0
        return remote(
            rs_send.at[half, n, index],
            rs_recv.at[half, n, index],
            r_send.at[k],
            r_recv.at[k],
            along(half, axis, 1 if index % 2 == 0 else -1),
        )

    def rs_start(half, n, index, value):
        rs_send[half, n, index] = value.astype(BF16)
        rs_copy(half, n, index).start()

    def rs_take(half, n, index):
        rs_copy(half, n, index).wait_recv()
        return rs_recv[half, n, index].astype(F32)

    def partial(half, d1, d2):
        o = block(half, d1, d2)
        rows = pl.ds(pl.multiple_of(o * SHARD + half * HALF, HALF), HALF)
        return jnp.dot(tok_t[rows, :], d_pair[o // 8], preferred_element_type=F32)

    def opposite(n):
        for half in (0, 1):
            value = partial(half, 2, OFFSETS[n])
            rs_start(half, n, 0, value[:QUARTER])
            rs_start(half, n, 1, value[QUARTER:])

    def sides(n):
        for half in (0, 1):
            up = partial(half, 1, OFFSETS[n])
            rs_start(half, n, 2, up[QUARTER:])
            part[n, half, 0] = up[:QUARTER]
            down = partial(half, -1, OFFSETS[n])
            rs_start(half, n, 3, down[:QUARTER])
            part[n, half, 1] = down[QUARTER:]

    def stay(n):
        for half in (0, 1):
            own = partial(half, 0, OFFSETS[n])
            part[n, half, 2] = own[:QUARTER]
            part[n, half, 3] = own[QUARTER:]

    def combine(n):
        for half in (0, 1):
            rs_start(half, n, 4, part[n, half, 0] + rs_take(half, n, 0))
            rs_start(half, n, 5, part[n, half, 1] + rs_take(half, n, 1))

    def finish(n):
        for half in (0, 1):
            top = part[n, half, 2] + rs_take(half, n, 3) + rs_take(half, n, 4)
            bottom = part[n, half, 3] + rs_take(half, n, 2) + rs_take(half, n, 5)
            if n == 0:
                rs_start(half, 4, 0, top)
                rs_start(half, 4, 1, bottom)
            if n == 1:
                rs_start(half, 4, 2, bottom)
                part[1, half, 2] = top
            if n == 2:
                rs_start(half, 4, 3, top)
                part[2, half, 3] = bottom
            if n == 3:
                top = top + rs_take(half, 4, 3) + rs_take(half, 4, 4)
                bottom = bottom + rs_take(half, 4, 2) + rs_take(half, 4, 5)
                z_send[half * HALF : half * HALF + QUARTER] = top.astype(BF16)
                z_send[half * HALF + QUARTER : (half + 1) * HALF] = bottom.astype(BF16)

    opposite(0)
    sides(0)
    opposite(1)
    sides(1)
    opposite(2)
    stay(0)
    combine(0)
    sides(2)
    opposite(3)
    combine(1)
    stay(1)
    stay(2)
    combine(2)
    finish(0)
    sides(3)
    combine(3)
    stay(3)
    finish(1)
    finish(2)
    for half in (0, 1):
        rs_start(half, 4, 4, part[1, half, 2] + rs_take(half, 4, 0))
        rs_start(half, 4, 5, part[2, half, 3] + rs_take(half, 4, 1))
    finish(3)

    per = SHARD // (2 * nz)

    def z_copy(i, k):
        to = (z + i) % nz
        its = core if k == 0 else other
        rows = pl.ds(pl.multiple_of((2 * to + its) * per, per), per)
        return remote(
            z_send.at[rows],
            z_recv.at[k, i],
            zs_sem.at[k, i],
            zr_sem.at[k, i],
            (2 * to + its, f),
        )

    def z_start(i, carry):
        away = (i + 1) // 2
        distance = nz // 2 + jnp.where(i % 2 == 0, away, -away)
        z_copy(distance, 0).start()
        z_copy(distance, 1).start()
        return carry

    def z_take(i, k):
        z_copy(i, k).wait_recv()
        return z_recv[k, i].astype(F32)

    def z_add(i, carry):
        return tuple(total + z_take(2 * i + n // 2, n % 2) for n, total in enumerate(carry))

    lax.fori_loop(0, nz - 1, z_start, 0)
    z_copy(0, 1).start()
    for copy in core_copies:
        copy.wait_send()
    for copy in ag_sent:
        copy.wait_send()
    for k in (0, 1):
        delta_copy(k).wait_send()
        for q in range(CHUNKS):
            swap_copy(k, q).wait_send()
            pass_copy(k, q).wait_send()

    def rs_done(n, carry):
        for half in (0, 1):
            for index in range(6):
                rs_copy(half, n, index).wait_send()
        return carry

    lax.fori_loop(0, 5, rs_done, 0)

    rows = pl.ds(pl.multiple_of((2 * z + core) * per, per), per)
    mine_sum = z_send[rows, :].astype(F32)
    sums = (mine_sum, z_take(0, 1), z_take(1, 0), z_take(1, 1))
    sums = lax.fori_loop(1, nz // 2, z_add, sums)
    factor = 1.0 / math.sqrt(nz * 2 * RING * RING * TOK)
    even = [jnp.where(parity == 0, sums[k], sums[2 + k]) * factor for k in (0, 1)]
    odd = [jnp.where(parity == 0, sums[2 + k], sums[k]) * factor for k in (0, 1)]
    out[:, :HD] = jnp.where(core == 0, even[0], even[1])
    out[:, HD : 2 * HD] = jnp.where(core == 0, odd[0], odd[1])
    out[:, 2 * HD : 3 * HD] = jnp.where(core == 0, even[1], even[0])
    out[:, 3 * HD :] = jnp.where(core == 0, odd[1], odd[0])

    def z_sent(i, carry):
        z_copy(i, 0).wait_send()
        z_copy(i, 1).wait_send()
        return carry

    z_copy(0, 1).wait_send()
    lax.fori_loop(1, nz, z_sent, 0)


def local(nz, counts, tokens, queries, values, out_grad, key_codes, key_scales):
    width = SHARD // nz
    return pl.pallas_call(
        functools.partial(kernel, nz),
        out_shape=jax.ShapeDtypeStruct((width // 2, 2 * HALF), F32),
        in_specs=[pl.BlockSpec(memory_space=pltpu.SMEM)]
        + [pl.BlockSpec(memory_space=pltpu.HBM)] * 6,
        out_specs=pl.BlockSpec(memory_space=pltpu.VMEM),
        scratch_shapes=[
            pltpu.VMEM((SHARD, HALF), BF16),
            pltpu.VMEM((2, SHARD), F32),
            pltpu.VMEM((2, 8, 128), jnp.int32),
            pltpu.VMEM((2 * TOK, 16 * SHARD), BF16),
            pltpu.VMEM((16 * SHARD, 4 * TOK), BF16),
            pltpu.VMEM((2 * TOK, QW), BF16),
            pltpu.VMEM((2 * TOK, HALF), BF16),
            pltpu.VMEM((2 * TOK, QW), BF16),
            pltpu.VMEM((2, 16, 2, HALF, HD), BF16),
            pltpu.VMEM((2, 2 * TOK, HD), F32),
            pltpu.VMEM((2, 2 * TOK, HD), BF16),
            pltpu.VMEM((2 * TOK, HD), BF16),
            pltpu.VMEM((2, 4 * TOK, HD), BF16),
            pltpu.VMEM((2, 2 * TOK, WIDE), BF16),
            pltpu.VMEM((4, 2, 4, QUARTER, HD), F32),
            pltpu.VMEM((2, 5, 6, QUARTER, HD), BF16),
            pltpu.VMEM((2, 5, 6, QUARTER, HD), BF16),
            pltpu.VMEM((SHARD, HD), BF16),
            pltpu.VMEM((2, nz, width // 2, HD), BF16),
            pltpu.SemaphoreType.DMA((6,)),
            pltpu.SemaphoreType.DMA((6,)),
            pltpu.SemaphoreType.DMA((6,)),
            pltpu.SemaphoreType.DMA((88,)),
            pltpu.SemaphoreType.DMA((88,)),
            pltpu.SemaphoreType.DMA((60,)),
            pltpu.SemaphoreType.DMA((60,)),
            pltpu.SemaphoreType.DMA((2, nz)),
            pltpu.SemaphoreType.DMA((2, nz)),
            pltpu.SemaphoreType.DMA((2 * CHUNKS,)),
            pltpu.SemaphoreType.DMA((2 * CHUNKS,)),
            pltpu.SemaphoreType.DMA((2 * CHUNKS,)),
            pltpu.SemaphoreType.DMA((2 * CHUNKS,)),
            pltpu.SemaphoreType.DMA((2,)),
            pltpu.SemaphoreType.DMA((2,)),
            pltpu.SemaphoreType.REGULAR((8,)),
        ],
        compiler_params=pltpu.CompilerParams(
            collective_id=0,
            has_side_effects=True,
            vmem_limit_bytes=62 * 1024 * 1024,
        ),
        cost_estimate=pl.CostEstimate(
            flops=2_300_000_000, bytes_accessed=6_000_000, transcendentals=140_000
        ),
    )(counts, tokens, queries, values, out_grad, key_codes, key_scales.T)


def solution(mesh):
    return jax.shard_map(
        functools.partial(local, mesh.shape["dp"] // 2),
        mesh=mesh,
        in_specs=(
            P(("dp", "fsdp")),
            P(("dp", "fsdp"), None),
            P(("dp", "fsdp"), None),
            P(("dp", "fsdp"), None),
            P(("dp", "fsdp"), None),
            P("fsdp", None),
            P("fsdp", None),
        ),
        out_specs=P(("fsdp", "dp"), None),
        check_vma=False,
    )
```

```python
import functools
import math

import jax
import jax.numpy as jnp
from jax import lax
from jax.experimental import pallas as pl
from jax.experimental.pallas import tpu as pltpu
from jax.sharding import PartitionSpec as P

MESH = pl.DeviceIdType.MESH
F32 = jnp.float32
BF16 = jnp.bfloat16
HD = 128
RING = 4
TOK = 128
MB = 32
SHARD = 512
HALF = 256
QUARTER = 128
GROUP = 8
QW = 2048
OFFSETS = (2, 1, -1, 0)
CHUNKS = 4
FROM = (0, 1024, 2048, 3584, 4096)
WIDE = 4096


def kernel(
    nz,
    counts,
    tokens,
    queries,
    values,
    out_grad,
    codes,
    scales,
    out,
    codes_v,
    scales_v,
    cnt,
    tok,
    tok_t,
    q2,
    v2,
    og2,
    wbuf,
    acc,
    keys,
    d_send,
    d_pair,
    tok_z,
    part,
    rs_send,
    rs_recv,
    z_send,
    z_recv,
    load_sem,
    core_send,
    core_recv,
    ag_send,
    ag_recv,
    r_send,
    r_recv,
    zs_sem,
    zr_sem,
    t_send,
    t_recv,
    f_send,
    f_recv,
    d_ssem,
    d_rsem,
    relay,
):
    dp = lax.axis_index("dp")
    f = lax.axis_index("fsdp")
    x, y = f // RING, f % RING
    z, core = dp // 2, dp % 2
    other = 1 - core
    partner = (2 * z + other, f)

    def wrap(v):
        return (v + 2 * RING) % RING

    def chip(dx, dy):
        return (dp, wrap(x + dx) * RING + wrap(y + dy))

    def along(half, axis, step):
        if half == axis:
            return chip(step, 0)
        return chip(0, step)

    def block(half, d1, d2):
        dx = d1 * (1 - half) + d2 * half
        dy = d2 * (1 - half) + d1 * half
        return wrap(x + dx) * RING + wrap(y + dy)

    def z_peer(i):
        return (((z + i) % nz) * 2 + core, f)

    parity = z % 2
    pair = (z_peer(nz + 1 - 2 * parity), z_peer(nz - 1 + 2 * parity))

    barrier = pltpu.get_barrier_semaphore()
    neighbours = [partner, chip(1, 0), chip(-1, 0), chip(0, 1), chip(0, -1), *pair]
    for device in neighbours:
        pl.semaphore_signal(barrier, inc=1, device_id=device, device_id_type=MESH)

    mine = pl.ds(pl.multiple_of(core * HALF, HALF), HALF)
    theirs = pl.ds(pl.multiple_of(other * HALF, HALF), HALF)
    mine_q = pl.ds(pl.multiple_of(core * QW, QW), QW)
    theirs_q = pl.ds(pl.multiple_of(other * QW, QW), QW)
    low, high = pl.ds(0, TOK), pl.ds(TOK, TOK)
    loads = [
        pltpu.make_async_copy(src, dst, load_sem.at[i])
        for i, (src, dst) in enumerate(
            [
                (codes.at[:, mine], codes_v),
                (scales, scales_v),
                (tokens, tok.at[low]),
                (queries.at[:, mine_q], q2.at[low]),
                (values.at[:, mine], v2.at[low]),
                (out_grad.at[:, mine_q], og2.at[low]),
            ]
        )
    ]
    for load in loads[:2]:
        load.start()
    loads[0].wait()
    loads[1].wait()
    scale = jnp.where(core == 0, scales_v[0:1], scales_v[1:2])
    scale = jnp.broadcast_to(scale, (HD, SHARD)).T
    left = (codes_v[:, :HD].astype(F32) * scale).astype(BF16)
    right = (codes_v[:, HD:].astype(F32) * scale).astype(BF16)
    for half in (0, 1):
        rows = slice(half * HALF, (half + 1) * HALF)
        wbuf[0, f, half] = jnp.where(parity == 0, right[rows], left[rows])
        wbuf[1, f, half] = jnp.where(parity == 0, left[rows], right[rows])

    for load in loads[2:]:
        load.start()
    pl.semaphore_wait(barrier, len(neighbours))

    def remote(src, dst, send, recv, device):
        return pltpu.make_async_remote_copy(
            src_ref=src,
            dst_ref=dst,
            send_sem=send,
            recv_sem=recv,
            device_id=device,
            device_id_type=MESH,
        )

    upper, lower = pl.ds(0, QUARTER), pl.ds(QUARTER, QUARTER)
    whole = pl.ds(0, HALF)
    ag_sent = []

    def ag_copy(p, half, index, o, rows, axis, step):
        k = (p * 2 + half) * 22 + index
        ref = wbuf.at[p, o, half, rows]
        return remote(ref, ref, ag_send.at[k], ag_recv.at[k], along(half, axis, step))

    def ag_start(*args):
        copy = ag_copy(*args)
        copy.start()
        ag_sent.append(copy)

    def ag_wait(p, half, index, rows):
        ag_copy(p, half, index, f, rows, 0, 1).wait_recv()

    FIRST = (0, -1, 1, 2)

    def both(p, half, index, d1, d2, axis):
        ag_start(p, half, index, block(half, d1, d2), whole, axis, 1)
        ag_start(p, half, index + 1, block(half, d1, d2), whole, axis, -1)

    def gather_start(p, axis):
        for half in (0, 1):
            both(p, half, 4 * axis, 0, 0, axis)

    gather_start(0, 0)
    gather_start(0, 1)
    def swap_copy(k, q):
        i = k * CHUNKS + q
        columns = pl.ds(k * WIDE + FROM[q], FROM[q + 1] - FROM[q])
        into = pl.ds(FROM[q], FROM[q + 1] - FROM[q])
        return remote(
            tokens.at[:, columns], tok_z.at[k, low, into], t_send.at[i], t_recv.at[i], pair[k]
        )

    for q in range(CHUNKS):
        for k in (0, 1):
            swap_copy(k, q).start()

    gather_start(1, 0)
    gather_start(1, 1)

    reach = [1 << r for r in range(nz.bit_length()) if 1 << r < nz // 2]

    def tell(r):
        pl.semaphore_signal(
            relay.at[2 * r], inc=1, device_id=z_peer(reach[r]), device_id_type=MESH
        )
        pl.semaphore_signal(
            relay.at[2 * r + 1], inc=1, device_id=z_peer(nz - reach[r]), device_id_type=MESH
        )

    def hear(r):
        pl.semaphore_wait(relay.at[2 * r], 1)
        pl.semaphore_wait(relay.at[2 * r + 1], 1)

    core_copies = [
        remote(src, dst, core_send.at[i], core_recv.at[i], partner)
        for i, (src, dst) in enumerate(
            [
                (tokens, tok.at[high]),
                (queries.at[:, theirs_q], q2.at[high]),
                (out_grad.at[:, theirs_q], og2.at[high]),
                (values.at[:, theirs], v2.at[high]),
                (cnt.at[0], cnt.at[1]),
            ]
        )
    ]
    for copy in core_copies[:4]:
        copy.start()

    def pass_copy(k, q):
        i = k * CHUNKS + q
        into = pl.ds(FROM[q], FROM[q + 1] - FROM[q])
        return remote(
            tok_z.at[k, low, into], tok_z.at[k, high, into], f_send.at[i], f_recv.at[i], partner
        )

    def pass_on(q):
        for k in (0, 1):
            swap_copy(k, q).wait_recv()
            pass_copy(k, q).start()

    def transpose_pair(q):
        for k in (0, 1):
            pass_copy(k, q).wait_recv()

        def body(i, carry):
            k = i // pieces
            at = FROM[q] + (i % pieces) * SHARD
            columns = pl.ds(pl.multiple_of(at, SHARD), SHARD)
            rows = pl.ds(pl.multiple_of(k * WIDE + at, SHARD), SHARD)
            tok_t[rows, 2 * TOK :] = tok_z[k, :, columns].T
            return carry

        pieces = (FROM[q + 1] - FROM[q]) // SHARD
        lax.fori_loop(0, 2 * pieces, body, 0)

    def project(p, *offsets):
        total = acc[p]
        for d1, d2 in offsets:
            for half in (0, 1):
                o = block(half, d1, d2)
                columns = pl.ds(pl.multiple_of(o * SHARD + half * HALF, HALF), HALF)
                total += jnp.dot(tok[:, columns], wbuf[p, o, half], preferred_element_type=F32)
        acc[p] = total

    def transpose(first, last):
        def body(k, carry):
            piece = pl.ds(pl.multiple_of(k * SHARD, SHARD), SHARD)
            tok_t[piece, : 2 * TOK] = tok[:, piece].T
            return carry

        lax.fori_loop(first, last, body, 0)

    def first_pass(p):
        for half in (0, 1):
            ag_wait(p, half, 0, whole)
            ag_start(p, half, 2, block(half, -1, 0), upper, 0, 1)
            ag_wait(p, half, 1, whole)
            ag_start(p, half, 3, block(half, 1, 0), lower, 0, -1)

    def second_start(p):
        for half in (0, 1):
            both(p, half, 8, -1, 0, 1)
            both(p, half, 12, 1, 0, 1)

    def first_end(p):
        for half in (0, 1):
            ag_wait(p, half, 2, upper)
            ag_wait(p, half, 3, lower)
            o = block(half, 2, 0)
            ag_start(p, half, 16, o, upper, 1, 1)
            ag_start(p, half, 17, o, lower, 1, -1)
            ag_start(p, half, 21, o, lower, 1, 1)
            ag_start(p, half, 20, o, upper, 1, -1)

    def second_pass(p, j):
        for half in (0, 1):
            base = 4 + 4 * j
            ag_wait(p, half, base, whole if j < 3 else upper)
            ag_start(p, half, base + 2, block(half, FIRST[j], -1), upper, 1, 1)
            ag_wait(p, half, base + 1, whole if j < 3 else lower)
            ag_start(p, half, base + 3, block(half, FIRST[j], 1), lower, 1, -1)

    def second_end(p, j):
        for half in (0, 1):
            ag_wait(p, half, 4 + 4 * j + 2, upper)
            ag_wait(p, half, 4 + 4 * j + 3, lower)

    def second_rest(p):
        for half in (0, 1):
            ag_wait(p, half, 20, upper)
            ag_wait(p, half, 21, lower)

    inverse = 1.0 / math.sqrt(HD)
    key_at = lax.broadcasted_iota(jnp.int32, (MB, GROUP * MB), 0)
    query_at = lax.broadcasted_iota(jnp.int32, (MB, GROUP * MB), 1) % MB
    seen = key_at <= query_at
    contract_last = (((1,), (1,)), ((), ()))

    def attend(p, first, last, result):
        head = (1 - parity) if p == 0 else parity
        columns = pl.ds(pl.multiple_of(head * HD, HD), HD)

        def group(ref, rows):
            return jnp.concatenate(
                [
                    ref[rows, pl.ds(pl.multiple_of((head * GROUP + g) * HD, HD), HD)]
                    for g in range(GROUP)
                ],
                axis=0,
            )

        def microbatch(m):
            rows = pl.ds(pl.multiple_of(m * MB, MB), MB)
            live = (m % 4) < cnt[m // 4][0:1]
            query = group(q2, rows)
            scores = lax.dot_general(
                keys[p, rows, :], query, contract_last, preferred_element_type=F32
            )
            weights = jnp.where(seen, jnp.exp(scores * inverse), 0.0)
            probs = weights / jnp.sum(weights, axis=0, keepdims=True)
            prob_grad = lax.dot_general(
                v2[rows, columns], group(og2, rows), contract_last, preferred_element_type=F32
            )
            row_delta = jnp.sum(probs * prob_grad, axis=0, keepdims=True)
            dscore = (probs * (prob_grad - row_delta)).astype(BF16)
            key_grad = jnp.dot(dscore, query, preferred_element_type=F32) * inverse
            result[rows, :] = jnp.where(live, key_grad, 0.0).astype(BF16)

        def body(i, carry):
            for m in range(4):
                microbatch(4 * i + m)
            return carry

        lax.fori_loop(first, last, body, 0)

    def delta_copy(k):
        return remote(d_send, d_pair.at[k, pl.ds(2 * TOK, 2 * TOK)], d_ssem.at[k], d_rsem.at[k], pair[k])

    tell(0)
    cnt[0] = jnp.full((8, 128), counts[0], jnp.int32)
    core_copies[4].start()
    acc[...] = jnp.zeros_like(acc)
    first_pass(0)
    second_start(0)
    second_pass(0, 0)
    hear(0)
    tell(1)
    loads[2].wait()
    core_copies[0].wait_recv()
    first_pass(1)
    transpose(0, 2)
    second_pass(1, 0)
    transpose(2, 4)
    first_end(0)
    second_start(1)
    project(0, (0, 0), (-1, 0), (1, 0), (0, -1), (0, 1))
    second_pass(0, 1)
    transpose(4, 6)
    second_pass(0, 2)
    hear(1)
    tell(2)
    pass_on(0)
    transpose(6, 8)
    first_end(1)
    project(0, (2, 0), (-1, -1), (-1, 1))
    second_pass(0, 3)
    second_end(0, 0)
    second_end(0, 1)
    project(0, (1, -1), (1, 1), (0, 2), (-1, 2))
    transpose(8, 10)
    pass_on(1)
    second_pass(1, 1)
    second_end(0, 2)
    second_pass(1, 2)
    second_rest(0)
    project(0, (1, 2), (2, -1), (2, 1))
    second_end(0, 3)
    project(0, (2, 2))
    keys[0] = acc[0].astype(BF16)
    for load in loads[3:]:
        load.wait()
    for copy in core_copies[1:]:
        copy.wait_recv()
    attend(0, 0, 1, d_send)
    second_pass(1, 3)
    attend(0, 1, 2, d_send)
    for k in (0, 1):
        delta_copy(k).start()
    pass_on(2)
    project(1, (0, 0), (-1, 0), (1, 0), (0, -1), (0, 1), (2, 0))
    second_end(1, 0)
    second_end(1, 1)
    project(1, (-1, -1), (-1, 1), (1, -1), (1, 1), (0, 2), (-1, 2))
    transpose(10, 16)
    hear(2)
    second_end(1, 2)
    second_rest(1)
    project(1, (1, 2), (2, -1), (2, 1))
    transpose_pair(0)
    transpose_pair(1)
    pass_on(3)
    transpose_pair(2)
    second_end(1, 3)
    project(1, (2, 2))
    keys[1] = acc[1].astype(BF16)
    attend(1, 0, 2, d_pair.at[0, pl.ds(0, 2 * TOK)])
    d_pair[1, : 2 * TOK] = d_pair[0, : 2 * TOK]
    transpose_pair(3)
    for k in (0, 1):
        delta_copy(k).wait_recv()

    def rs_copy(half, n, index):
        k = (half * 5 + n) * 6 + index
        axis = 1 if isinstance(n, int) and n == 4 else 0
        return remote(
            rs_send.at[half, n, index],
            rs_recv.at[half, n, index],
            r_send.at[k],
            r_recv.at[k],
            along(half, axis, 1 if index % 2 == 0 else -1),
        )

    def rs_start(half, n, index, value):
        rs_send[half, n, index] = value.astype(BF16)
        rs_copy(half, n, index).start()

    def rs_take(half, n, index):
        rs_copy(half, n, index).wait_recv()
        return rs_recv[half, n, index].astype(F32)

    def partial(half, d1, d2):
        o = block(half, d1, d2)
        rows = pl.ds(pl.multiple_of(o * SHARD + half * HALF, HALF), HALF)
        return jnp.dot(tok_t[rows, :], d_pair[o // 8], preferred_element_type=F32)

    def opposite(n):
        for half in (0, 1):
            value = partial(half, 2, OFFSETS[n])
            rs_start(half, n, 0, value[:QUARTER])
            rs_start(half, n, 1, value[QUARTER:])

    def sides(n):
        for half in (0, 1):
            up = partial(half, 1, OFFSETS[n])
            rs_start(half, n, 2, up[QUARTER:])
            part[n, half, 0] = up[:QUARTER]
            down = partial(half, -1, OFFSETS[n])
            rs_start(half, n, 3, down[:QUARTER])
            part[n, half, 1] = down[QUARTER:]

    def stay(n):
        for half in (0, 1):
            own = partial(half, 0, OFFSETS[n])
            part[n, half, 2] = own[:QUARTER]
            part[n, half, 3] = own[QUARTER:]

    def combine(n):
        for half in (0, 1):
            rs_start(half, n, 4, part[n, half, 0] + rs_take(half, n, 0))
            rs_start(half, n, 5, part[n, half, 1] + rs_take(half, n, 1))

    def finish(n):
        for half in (0, 1):
            top = part[n, half, 2] + rs_take(half, n, 3) + rs_take(half, n, 4)
            bottom = part[n, half, 3] + rs_take(half, n, 2) + rs_take(half, n, 5)
            if n == 0:
                rs_start(half, 4, 0, top)
                rs_start(half, 4, 1, bottom)
            if n == 1:
                rs_start(half, 4, 2, bottom)
                part[1, half, 2] = top
            if n == 2:
                rs_start(half, 4, 3, top)
                part[2, half, 3] = bottom
            if n == 3:
                top = top + rs_take(half, 4, 3) + rs_take(half, 4, 4)
                bottom = bottom + rs_take(half, 4, 2) + rs_take(half, 4, 5)
                z_send[half * HALF : half * HALF + QUARTER] = top.astype(BF16)
                z_send[half * HALF + QUARTER : (half + 1) * HALF] = bottom.astype(BF16)

    opposite(0)
    sides(0)
    opposite(1)
    sides(1)
    opposite(2)
    stay(0)
    combine(0)
    sides(2)
    opposite(3)
    combine(1)
    stay(1)
    stay(2)
    combine(2)
    finish(0)
    sides(3)
    combine(3)
    stay(3)
    finish(1)
    finish(2)
    for half in (0, 1):
        rs_start(half, 4, 4, part[1, half, 2] + rs_take(half, 4, 0))
        rs_start(half, 4, 5, part[2, half, 3] + rs_take(half, 4, 1))
    finish(3)

    per = SHARD // (2 * nz)

    def z_copy(i, k):
        to = (z + i) % nz
        its = core if k == 0 else other
        rows = pl.ds(pl.multiple_of((2 * to + its) * per, per), per)
        return remote(
            z_send.at[rows],
            z_recv.at[k, i],
            zs_sem.at[k, i],
            zr_sem.at[k, i],
            (2 * to + its, f),
        )

    def z_start(i, carry):
        away = (i + 1) // 2
        distance = nz // 2 + jnp.where(i % 2 == 0, away, -away)
        z_copy(distance, 0).start()
        z_copy(distance, 1).start()
        return carry

    def z_take(i, k):
        z_copy(i, k).wait_recv()
        return z_recv[k, i].astype(F32)

    def z_add(i, carry):
        return tuple(total + z_take(2 * i + n // 2, n % 2) for n, total in enumerate(carry))

    lax.fori_loop(0, nz - 1, z_start, 0)
    z_copy(0, 1).start()
    for copy in core_copies:
        copy.wait_send()
    for copy in ag_sent:
        copy.wait_send()
    for k in (0, 1):
        delta_copy(k).wait_send()
        for q in range(CHUNKS):
            swap_copy(k, q).wait_send()
            pass_copy(k, q).wait_send()

    def rs_done(n, carry):
        for half in (0, 1):
            for index in range(6):
                rs_copy(half, n, index).wait_send()
        return carry

    lax.fori_loop(0, 5, rs_done, 0)

    rows = pl.ds(pl.multiple_of((2 * z + core) * per, per), per)
    mine_sum = z_send[rows, :].astype(F32)
    sums = (mine_sum, z_take(0, 1), z_take(1, 0), z_take(1, 1))
    sums = lax.fori_loop(1, nz // 2, z_add, sums)
    factor = 1.0 / math.sqrt(nz * 2 * RING * RING * TOK)
    even = [jnp.where(parity == 0, sums[k], sums[2 + k]) * factor for k in (0, 1)]
    odd = [jnp.where(parity == 0, sums[2 + k], sums[k]) * factor for k in (0, 1)]
    out[:, :HD] = jnp.where(core == 0, even[0], even[1])
    out[:, HD : 2 * HD] = jnp.where(core == 0, odd[0], odd[1])
    out[:, 2 * HD : 3 * HD] = jnp.where(core == 0, even[1], even[0])
    out[:, 3 * HD :] = jnp.where(core == 0, odd[1], odd[0])

    def z_sent(i, carry):
        z_copy(i, 0).wait_send()
        z_copy(i, 1).wait_send()
        return carry

    z_copy(0, 1).wait_send()
    lax.fori_loop(1, nz, z_sent, 0)


def local(nz, counts, tokens, queries, values, out_grad, key_codes, key_scales):
    width = SHARD // nz
    return pl.pallas_call(
        functools.partial(kernel, nz),
        out_shape=jax.ShapeDtypeStruct((width // 2, 2 * HALF), F32),
        in_specs=[pl.BlockSpec(memory_space=pltpu.SMEM)]
        + [pl.BlockSpec(memory_space=pltpu.HBM)] * 6,
        out_specs=pl.BlockSpec(memory_space=pltpu.VMEM),
        scratch_shapes=[
            pltpu.VMEM((SHARD, HALF), BF16),
            pltpu.VMEM((2, SHARD), F32),
            pltpu.VMEM((2, 8, 128), jnp.int32),
            pltpu.VMEM((2 * TOK, 16 * SHARD), BF16),
            pltpu.VMEM((16 * SHARD, 4 * TOK), BF16),
            pltpu.VMEM((2 * TOK, QW), BF16),
            pltpu.VMEM((2 * TOK, HALF), BF16),
            pltpu.VMEM((2 * TOK, QW), BF16),
            pltpu.VMEM((2, 16, 2, HALF, HD), BF16),
            pltpu.VMEM((2, 2 * TOK, HD), F32),
            pltpu.VMEM((2, 2 * TOK, HD), BF16),
            pltpu.VMEM((2 * TOK, HD), BF16),
            pltpu.VMEM((2, 4 * TOK, HD), BF16),
            pltpu.VMEM((2, 2 * TOK, WIDE), BF16),
            pltpu.VMEM((4, 2, 4, QUARTER, HD), F32),
            pltpu.VMEM((2, 5, 6, QUARTER, HD), BF16),
            pltpu.VMEM((2, 5, 6, QUARTER, HD), BF16),
            pltpu.VMEM((SHARD, HD), BF16),
            pltpu.VMEM((2, nz, width // 2, HD), BF16),
            pltpu.SemaphoreType.DMA((6,)),
            pltpu.SemaphoreType.DMA((6,)),
            pltpu.SemaphoreType.DMA((6,)),
            pltpu.SemaphoreType.DMA((88,)),
            pltpu.SemaphoreType.DMA((88,)),
            pltpu.SemaphoreType.DMA((60,)),
            pltpu.SemaphoreType.DMA((60,)),
            pltpu.SemaphoreType.DMA((2, nz)),
            pltpu.SemaphoreType.DMA((2, nz)),
            pltpu.SemaphoreType.DMA((2 * CHUNKS,)),
            pltpu.SemaphoreType.DMA((2 * CHUNKS,)),
            pltpu.SemaphoreType.DMA((2 * CHUNKS,)),
            pltpu.SemaphoreType.DMA((2 * CHUNKS,)),
            pltpu.SemaphoreType.DMA((2,)),
            pltpu.SemaphoreType.DMA((2,)),
            pltpu.SemaphoreType.REGULAR((8,)),
        ],
        compiler_params=pltpu.CompilerParams(
            collective_id=0,
            has_side_effects=True,
            vmem_limit_bytes=62 * 1024 * 1024,
        ),
        cost_estimate=pl.CostEstimate(
            flops=2_300_000_000, bytes_accessed=6_000_000, transcendentals=140_000
        ),
    )(counts, tokens, queries, values, out_grad, key_codes, key_scales.T)


def solution(mesh):
    return jax.shard_map(
        functools.partial(local, mesh.shape["dp"] // 2),
        mesh=mesh,
        in_specs=(
            P(("dp", "fsdp")),
            P(("dp", "fsdp"), None),
            P(("dp", "fsdp"), None),
            P(("dp", "fsdp"), None),
            P(("dp", "fsdp"), None),
            P("fsdp", None),
            P("fsdp", None),
        ),
        out_specs=P(("fsdp", "dp"), None),
        check_vma=False,
    )
```
